512 devices in a mesh: seq: 64 (over z, y), head: 8 (over x, core).
Axes of the slice: x: 4, y: 4, z: 16, core: 2. Of those that a mesh axis runs over, the one named last changes fastest.
Arguments:
- queries: bfloat16 [32768, 4096], P(('seq', 'head')), may hold values from -25 to 25
- key_rows: bfloat16 [32768, 4096], P(('seq', 'head')), may hold values from -6 to 6
- value_rows: bfloat16 [32768, 4096], P(('seq', 'head')), may hold values from -6 to 6
- out_grad: bfloat16 [32768, 4096], P(('seq', 'head')), may hold values from -6 to 6
- doc_ids: int32 [32768], replicated, may hold values from 0 to 15, never falling along the last dimension, each value on 1 to 4096 neighbouring positions
- picks: int32 [64, 32, 2], P('seq', 'head'), may hold values from 1 to 3, as said below
Outputs:
- attn_out: bfloat16 [32768, 4096], P(('seq', 'head'))
- query_grad: bfloat16 [32768, 4096], P(('seq', 'head'))
- key_grad: bfloat16 [32768, 4096], P(('seq', 'head'))
- value_grad: bfloat16 [32768, 4096], P(('seq', 'head'))
The draws below stay inside these ranges and needn't reach their ends.
Inputs may be any that keep to these rules, and one draw needn't show every extreme that they name: `doc_ids`: never falling along the tokens; each document is at most 4096 tokens, one exactly that long. `picks`: for each block and head, 2 different offsets.
All inputs are finite; a program needn't handle non-finite values.
Results may differ from the reference program's by a relative error of at most 0.027.
Values may be sent and summed in bfloat16 or wider, within the bound.
No kernel may reach another device: no remote copies, remote signals or barrier semaphores. Data moves between devices by JAX's collectives and lax.ppermute only.
A program may use at most 128 MiB of HBM per device.

```python
import math
import jax
import jax.numpy as jnp
import numpy as np
from jax import lax

HEADS = 32
HEAD_DIM = 128
D = 4096
BLOCK = 512
TOPK = 2
REACH = 3
TOK_DEV = 512
TOKENS = 32768
NBLK = 64
DOCS = 16
N_SEQ = 64


def draw_queries(key, part):
    key = jax.random.fold_in(key, 1)
    return jnp.clip(jax.random.normal(key, (TOKENS, D), jnp.float32), -6.0, 6.0).astype(jnp.bfloat16)


def draw_key_rows(key, part):
    key = jax.random.fold_in(key, 2)
    return jnp.clip(jax.random.normal(key, (TOKENS, D), jnp.float32), -6.0, 6.0).astype(jnp.bfloat16)


def draw_picks(key, part):
    key = jax.random.fold_in(key, 3)
    raw = jax.random.randint(key, (NBLK, HEADS, REACH), 0, 1048576)
    ranked = raw * REACH + jnp.arange(REACH, dtype=jnp.int32)
    order = jnp.argsort(ranked, axis=-1)
    return (order[..., :TOPK] + 1).astype(jnp.int32)


def block_levels(stream_key, shape, shards, smallest, largest):
    gain = 1.0
    for position, parts in shards:
        steps = jax.random.uniform(jax.random.fold_in(jax.random.fold_in(stream_key, 6), position), (parts,), jnp.float32, smallest / len(shards), largest / len(shards))
        gain = gain * jnp.repeat(jnp.exp(steps), shape[position] // parts).reshape((-1,) + (1,) * (len(shape) - 1 - position))
    return gain


def length_profile(number_of, total, limit, lean):
    loads = [(1 << 20) // math.isqrt(grade ** lean) + 1 for grade in range(2, number_of + 1)]
    rest, counts = total - limit - (number_of - 1), [1] * (number_of - 1)
    while rest > 0:
        candidates = [i for i in range(number_of - 1) if counts[i] < limit]
        mass, budget = sum([loads[i] for i in candidates]), rest
        for i in candidates:
            addition = min(limit - counts[i], max(1, budget * loads[i] // mass), rest)
            counts[i] = counts[i] + addition
            rest = rest - addition
    return np.array([limit] + counts)


def ragged_sizes(stream_key, number_of, total, most, skew):
    if number_of == 2:
        one = jax.random.randint(stream_key, (), max(1, total - most), min(most, total - 1) + 1)
        return jnp.stack([one, total - one])
    lengths = jnp.asarray(length_profile(number_of, total, most, skew), jnp.int32)
    couples = (number_of - 1) // 2
    giver, sink = lengths[1:1 + 2 * couples:2], lengths[2:2 + 2 * couples:2]
    slack = jnp.minimum(giver - 1, most - sink)
    moved = jax.random.randint(jax.random.fold_in(stream_key, 1), (couples,), 0, 1 << 20) % (slack + 1)
    lengths = lengths.at[1:1 + 2 * couples:2].set(giver - moved).at[2:2 + 2 * couples:2].set(sink + moved)
    return lengths[jax.random.permutation(jax.random.fold_in(stream_key, 2), number_of)]


def normal_values(own_key, extent, width, bound, shards=(), held_as=jnp.bfloat16):
    values = jax.random.normal(own_key, extent, jnp.float32) * width
    if len(shards) > 0:
        values = block_levels(own_key, extent, shards, -0.22, 0.18) * values
    return jnp.clip(values, min=-bound, max=bound).astype(held_as)


def setup_inputs(seed: int = 0) -> dict:
    arg_keys = jax.random.split(jax.random.key(seed), 7)
    return {
        "queries": draw_queries(jax.random.fold_in(arg_keys[6], 71), 0),
        "key_rows": draw_key_rows(jax.random.fold_in(arg_keys[6], 71), 0),
        "value_rows": normal_values(arg_keys[2], (TOKENS, D), 1.0, 6.0, ((0, 512),)),
        "out_grad": normal_values(arg_keys[3], (TOKENS, D), 1.0, 6.0, ((0, 512),)),
        "doc_ids": jnp.searchsorted(jnp.cumsum(ragged_sizes(arg_keys[4], DOCS, TOKENS, 8 * BLOCK, 0)), jnp.arange(TOKENS), side="right").astype(jnp.int32),
        "picks": draw_picks(jax.random.fold_in(arg_keys[6], 71), 0),
    }


NEGATIVE = -1.0e30


def block_masks(picks_block, own_index, docs_query, docs_window):
    head_count = picks_block.shape[0]
    slot_count = docs_window.shape[0]
    block_rows = docs_query.shape[0]
    chosen = jnp.concatenate([own_index - picks_block, jnp.full((head_count, 1), own_index, jnp.int32)], axis=1).astype(jnp.int32)
    onehot = chosen[:, :, None] == jnp.arange(slot_count, dtype=jnp.int32)[None, None, :]
    docs_chosen = docs_window[chosen]
    key_count = chosen.shape[1]
    causal = jnp.arange(block_rows)[None, :] <= jnp.arange(block_rows)[:, None]
    earlier = jnp.arange(key_count) < key_count - 1
    allowed = jnp.logical_or(earlier[None, :, None], causal[:, None, :])
    same_doc = docs_query[None, :, None, None] == docs_chosen[:, None, :, :]
    return onehot, jnp.logical_and(same_doc, allowed[None])


def choose_rows(onehot, window):
    return jnp.einsum('hkw,wbhe->hkbe', onehot.astype(jnp.float32), window.astype(jnp.float32))


def masked_scores(query_head, keys_head, mask_head, score_scale):
    scores = jnp.einsum('be,kce->bkc', query_head.astype(jnp.float32), keys_head.astype(jnp.float32)) * score_scale
    return jnp.where(mask_head, scores, NEGATIVE)


def forward_heads(query_block, keys_chosen, values_chosen, allowed_mask, score_scale):
    def one_head(pieces):
        query_head, keys_head, values_head, mask_head = pieces
        scores = masked_scores(query_head, keys_head, mask_head, score_scale)
        row_max = jnp.max(scores, axis=(1, 2), keepdims=True)
        row_total = jnp.sum(jnp.exp(scores - row_max), axis=(1, 2), keepdims=True)
        log_total = row_max + jnp.log(row_total)
        probs_low = jnp.exp(scores - log_total).astype(jnp.bfloat16)
        result = jnp.einsum('bkc,kce->be', probs_low.astype(jnp.float32), values_head.astype(jnp.float32)).astype(jnp.bfloat16)
        return result, log_total[:, 0, 0]

    results, logs = lax.map(one_head, (jnp.swapaxes(query_block, 0, 1), keys_chosen, values_chosen, allowed_mask))
    return jnp.swapaxes(results, 0, 1), logs


def backward_heads(query_block, grad_block, out_block, log_block, keys_chosen, values_chosen, allowed_mask, onehot, score_scale):
    def one_head(pieces):
        query_head, grad_head, out_head, log_head, keys_head, values_head, mask_head, place_head = pieces
        scores = masked_scores(query_head, keys_head, mask_head, score_scale)
        probs_full = jnp.exp(scores - log_head[:, None, None])
        probs_low = probs_full.astype(jnp.bfloat16)
        delta = jnp.sum(grad_head.astype(jnp.float32) * out_head.astype(jnp.float32), axis=1)
        prob_grad = jnp.einsum('be,kce->bkc', grad_head.astype(jnp.float32), values_head.astype(jnp.float32))
        score_grad = (probs_full * (prob_grad - delta[:, None, None]) * score_scale).astype(jnp.bfloat16)
        query_part = jnp.einsum('bkc,kce->be', score_grad.astype(jnp.float32), keys_head.astype(jnp.float32))
        key_part = jnp.einsum('bkc,be->kce', score_grad.astype(jnp.float32), query_head.astype(jnp.float32))
        value_part = jnp.einsum('bkc,be->kce', probs_low.astype(jnp.float32), grad_head.astype(jnp.float32))
        placing = place_head.astype(jnp.float32)
        key_slots = jnp.einsum('kw,kce->wce', placing, key_part, precision=lax.Precision.HIGHEST)
        value_slots = jnp.einsum('kw,kce->wce', placing, value_part, precision=lax.Precision.HIGHEST)
        return query_part, key_slots, value_slots

    query_parts, key_slots, value_slots = lax.map(one_head, (jnp.swapaxes(query_block, 0, 1), jnp.swapaxes(grad_block, 0, 1), jnp.swapaxes(out_block, 0, 1), log_block, keys_chosen, values_chosen, allowed_mask, onehot))
    return jnp.swapaxes(query_parts, 0, 1), jnp.transpose(key_slots, (1, 2, 0, 3)), jnp.transpose(value_slots, (1, 2, 0, 3))


def reference(queries, key_rows, value_rows, out_grad, doc_ids, picks):
    block_count = TOK_DEV // BLOCK
    shifts = (REACH + block_count - 1) // block_count
    slot_count = (shifts + 1) * block_count
    feature_width = HEADS * HEAD_DIM
    pad_rows = shifts * TOK_DEV
    score_scale = HEAD_DIM ** -0.5

    def padded(array):
        zeros = jnp.zeros((pad_rows, feature_width), array.dtype)
        return jnp.concatenate([zeros, array], axis=0).reshape(-1, BLOCK, HEADS, HEAD_DIM)

    keys_pad = padded(key_rows)
    values_pad = padded(value_rows)
    docs_pad = jnp.concatenate([jnp.full((pad_rows,), -1, jnp.int32), doc_ids.astype(jnp.int32)])
    query_dev = queries.reshape(N_SEQ, block_count, BLOCK, HEADS, HEAD_DIM)
    grad_dev = out_grad.reshape(N_SEQ, block_count, BLOCK, HEADS, HEAD_DIM)
    picks_dev = picks.reshape(N_SEQ, block_count, HEADS, TOPK)

    def device_step(totals, pieces):
        key_acc, value_acc = totals
        seq_index, query_here, grad_here, picks_here = pieces
        first_block = (seq_index * block_count).astype(jnp.int32)
        key_window = lax.dynamic_slice_in_dim(keys_pad, first_block, slot_count, 0)
        value_window = lax.dynamic_slice_in_dim(values_pad, first_block, slot_count, 0)
        docs_window = lax.dynamic_slice_in_dim(docs_pad, (seq_index * TOK_DEV).astype(jnp.int32), slot_count * BLOCK, 0).reshape(slot_count, BLOCK)
        key_sum = jnp.zeros((slot_count, BLOCK, HEADS, HEAD_DIM), jnp.float32)
        value_sum = jnp.zeros((slot_count, BLOCK, HEADS, HEAD_DIM), jnp.float32)
        out_blocks = []
        query_blocks = []
        for local in range(block_count):
            own_index = shifts * block_count + local
            onehot, allowed_mask = block_masks(picks_here[local], own_index, docs_window[own_index], docs_window)
            keys_chosen = choose_rows(onehot, key_window)
            values_chosen = choose_rows(onehot, value_window)
            out_block, log_block = forward_heads(query_here[local], keys_chosen, values_chosen, allowed_mask, score_scale)
            query_part, key_slots, value_slots = backward_heads(query_here[local], grad_here[local], out_block, log_block, keys_chosen, values_chosen, allowed_mask, onehot, score_scale)
            key_sum = key_sum + key_slots
            value_sum = value_sum + value_slots
            out_blocks.append(out_block)
            query_blocks.append(query_part.astype(jnp.bfloat16))
        key_low = lax.optimization_barrier(key_sum.astype(jnp.bfloat16)).astype(jnp.float32)
        value_low = lax.optimization_barrier(value_sum.astype(jnp.bfloat16)).astype(jnp.float32)
        key_acc = lax.dynamic_update_slice_in_dim(key_acc, lax.dynamic_slice_in_dim(key_acc, first_block, slot_count, 0) + key_low, first_block, 0)
        value_acc = lax.dynamic_update_slice_in_dim(value_acc, lax.dynamic_slice_in_dim(value_acc, first_block, slot_count, 0) + value_low, first_block, 0)
        return (key_acc, value_acc), (jnp.stack(out_blocks), jnp.stack(query_blocks))

    start_totals = (jnp.zeros(keys_pad.shape, jnp.float32), jnp.zeros(values_pad.shape, jnp.float32))
    (key_acc, value_acc), (outs_all, query_all) = lax.scan(device_step, start_totals, (jnp.arange(N_SEQ, dtype=jnp.int32), query_dev, grad_dev, picks_dev))
    attn_out = outs_all.reshape(TOKENS, feature_width)
    query_grad = query_all.reshape(TOKENS, feature_width)
    key_grad = key_acc[shifts * block_count:].reshape(TOKENS, feature_width).astype(jnp.bfloat16)
    value_grad = value_acc[shifts * block_count:].reshape(TOKENS, feature_width).astype(jnp.bfloat16)
    return attn_out, query_grad, key_grad, value_grad
```

```python
import functools
import math

import jax
import jax.numpy as jnp
from jax import lax
from jax.experimental import pallas as pl
from jax.experimental.pallas import tpu as pltpu
from jax.sharding import Mesh
from jax.sharding import PartitionSpec as P

HEADS = 32
HEAD_DIM = 128
BLOCK = 512
REACH = 3
GROUP = 4
DOCS = 16
WINDOW = GROUP + REACH
CHUNK = 64
PER_BLOCK = BLOCK // CHUNK
NEGATIVE = -1e30
SCALE = HEAD_DIM ** (-0.5)
SCALE_LOG2 = SCALE * math.log2(math.e)

NT = (((1,), (1,)), ((), ()))
NN = (((1,), (0,)), ((), ()))


def dot(a, b, dims=NN):
    return lax.dot_general(a, b, dims, preferred_element_type=jnp.float32)


def attend(
    picks, docs, kv, halo, qd, od, dkv, back, keys, values, keys_t, values_t, key_sum, value_sum
):
    bf16 = jnp.bfloat16
    docs_t = jnp.transpose(docs[...])
    lane = lax.broadcasted_iota(jnp.int32, (128, 128), 1).astype(jnp.float32)

    def marks(row):
        return jnp.broadcast_to(docs_t[:, row : row + 1], (128, 128)) == lane

    for b in range(WINDOW):
        rows = pl.ds(b * BLOCK, BLOCK)
        source, at = (halo, b) if b < REACH else (kv, b - REACH)
        at = pl.ds(at * PER_BLOCK, PER_BLOCK)
        key = source[at, 0].reshape(BLOCK, HEAD_DIM)
        value = source[at, 1].reshape(BLOCK, HEAD_DIM)
        keys[rows, :HEAD_DIM] = key
        values[rows, :] = value
        keys_t[b] = jnp.transpose(key)
        values_t[b, :HEAD_DIM] = jnp.transpose(value)
        values_t[b, HEAD_DIM:] = jnp.ones((16, BLOCK), bf16)
        for part in range(4):
            row = b * 4 + part
            keys[pl.ds(row * 128, 128), HEAD_DIM:] = jnp.where(marks(row), 1.0, 0.0).astype(bf16)
    key_sum[...] = jnp.zeros_like(key_sum)
    value_sum[...] = jnp.zeros_like(value_sum)

    causal = lax.broadcasted_iota(jnp.int32, (BLOCK, BLOCK), 0) <= lax.broadcasted_iota(
        jnp.int32, (BLOCK, BLOCK), 1
    )
    for j in range(GROUP):
        own = REACH + j
        at = pl.ds(j * PER_BLOCK, PER_BLOCK)
        query = qd[at, 0].reshape(BLOCK, HEAD_DIM)
        grad = qd[at, 1].reshape(BLOCK, HEAD_DIM)
        bias = [
            jnp.where(jnp.logical_or(marks(own * 4 + part), lane > DOCS), 0.0, NEGATIVE)
            for part in range(4)
        ]
        query_wide = jnp.concatenate([query, jnp.concatenate(bias, axis=0).astype(bf16)], axis=1)
        slots = [own - picks[2 * j], own - picks[2 * j + 1], own]
        rows = [pl.ds(pl.multiple_of(s * BLOCK, BLOCK), BLOCK) for s in slots]
        scores = [dot(keys[r, :], query_wide, NT) for r in rows]
        scores[2] = jnp.where(causal, scores[2], NEGATIVE)
        top = functools.reduce(
            jnp.maximum, [jnp.max(s, axis=0, keepdims=True) for s in scores]
        )
        top = top * SCALE_LOG2
        probs = [jnp.exp2(s * SCALE_LOG2 - top).astype(bf16) for s in scores]
        result = sum(dot(values_t[s], p) for s, p in zip(slots, probs))
        inverse = 1.0 / result[HEAD_DIM : HEAD_DIM + 1]
        out_t = result[:HEAD_DIM] * inverse
        od[at, 0] = jnp.transpose(out_t).astype(bf16).reshape(PER_BLOCK, CHUNK, HEAD_DIM)
        grad_full = grad.astype(jnp.float32)
        delta = jnp.sum(jnp.transpose(grad_full) * out_t, axis=0, keepdims=True)
        inverse_rows = jnp.transpose(jnp.broadcast_to(inverse, (HEAD_DIM, BLOCK)))
        grad_low = (grad_full * inverse_rows).astype(bf16)
        query_low = (query.astype(jnp.float32) * (inverse_rows * SCALE)).astype(bf16)
        query_sum = None
        for s, r, p in zip(slots, rows, probs):
            prob_grad = dot(values[r, :], grad, NT)
            score_grad = (p.astype(jnp.float32) * (prob_grad - delta)).astype(bf16)
            part = dot(keys_t[s], score_grad)
            query_sum = part if query_sum is None else query_sum + part
            key_sum[r, :] += dot(score_grad, query_low)
            value_sum[r, :] += dot(p, grad_low)
        query_sum = query_sum * (inverse * SCALE)
        od[at, 1] = jnp.transpose(query_sum).astype(bf16).reshape(PER_BLOCK, CHUNK, HEAD_DIM)

    split = REACH * BLOCK
    for target, begin, rows in ((back, 0, split), (dkv, split, GROUP * BLOCK)):
        shape = (rows // CHUNK, CHUNK, HEAD_DIM)
        target[:, 0] = key_sum[begin : begin + rows].astype(bf16).reshape(shape)
        target[:, 1] = value_sum[begin : begin + rows].astype(bf16).reshape(shape)


def attention(picks, docs, kv, halo, qd):
    low = jnp.bfloat16
    pairs = 3 * GROUP * BLOCK * BLOCK
    vmem = pl.BlockSpec(memory_space=pltpu.VMEM)
    return pl.pallas_call(
        attend,
        out_shape=(
            jax.ShapeDtypeStruct(qd.shape, low),
            jax.ShapeDtypeStruct(kv.shape, low),
            jax.ShapeDtypeStruct(halo.shape, low),
        ),
        in_specs=[pl.BlockSpec(memory_space=pltpu.SMEM)] + [vmem] * 4,
        out_specs=(vmem,) * 3,
        scratch_shapes=[
            pltpu.VMEM((WINDOW * BLOCK, 2 * HEAD_DIM), low),
            pltpu.VMEM((WINDOW * BLOCK, HEAD_DIM), low),
            pltpu.VMEM((WINDOW, HEAD_DIM, BLOCK), low),
            pltpu.VMEM((WINDOW, HEAD_DIM + 16, BLOCK), low),
            pltpu.VMEM((WINDOW * BLOCK, HEAD_DIM), jnp.float32),
            pltpu.VMEM((WINDOW * BLOCK, HEAD_DIM), jnp.float32),
        ],
        compiler_params=pltpu.CompilerParams(vmem_limit_bytes=56 * 1024 * 1024),
        cost_estimate=pl.CostEstimate(
            flops=12 * pairs * HEAD_DIM,
            bytes_accessed=6 * 1024 * 1024,
            transcendentals=pairs,
        ),
        name="attend",
    )(picks, docs, kv, halo, qd)


def per_device(queries, key_rows, value_rows, out_grad, doc_ids, picks):
    plane = lax.axis_index("z")
    forward = [(i, i + 1) for i in range(lax.axis_size("z") - 1)]
    backward = [(i + 1, i) for i in range(lax.axis_size("z") - 1)]

    def to_heads(first, second):
        both = jnp.stack([first, second]).reshape(2, CHUNK, PER_BLOCK, GROUP, HEAD_DIM)
        both = jnp.transpose(both, (3, 2, 0, 1, 4)).reshape(HEADS, 2, CHUNK, HEAD_DIM)
        return lax.all_to_all(both, ("y", "h"), split_axis=0, concat_axis=0)

    def to_rows(both):
        both = lax.all_to_all(both, ("y", "h"), split_axis=0, concat_axis=0)
        both = both.reshape(GROUP, PER_BLOCK, 2, CHUNK, HEAD_DIM)
        both = jnp.transpose(both, (2, 3, 1, 0, 4)).reshape(2, CHUNK, HEADS * HEAD_DIM)
        return both[0], both[1]

    kv = to_heads(key_rows, value_rows)
    halo = lax.ppermute(kv[PER_BLOCK:], "z", forward)
    qd = to_heads(queries, out_grad)

    picks_plane = lax.all_gather(picks, "y", axis=0, tiled=True)
    picks_here = lax.dynamic_index_in_dim(picks_plane, lax.axis_index("y"), 1, False).reshape(-1)
    docs_pad = jnp.concatenate([jnp.full((REACH * BLOCK,), DOCS, jnp.int32), doc_ids])
    docs = lax.dynamic_slice_in_dim(docs_pad, plane * (GROUP * BLOCK), WINDOW * BLOCK, 0)
    docs = jnp.pad(docs.astype(jnp.float32).reshape(WINDOW * 4, 128), ((0, 4), (0, 0)))

    od, dkv, back = attention(picks_here, docs, kv, halo, qd)
    back = lax.ppermute(back, "z", backward)
    attn_out, query_grad = to_rows(od)
    back = jnp.pad(back, ((PER_BLOCK, 0), (0, 0), (0, 0), (0, 0)))
    dkv = (dkv.astype(jnp.float32) + back.astype(jnp.float32)).astype(jnp.bfloat16)
    key_grad, value_grad = to_rows(dkv)
    return attn_out, query_grad, key_grad, value_grad


def solution(mesh):
    planes = mesh.shape["seq"] // GROUP
    parts = Mesh(mesh.devices.reshape(planes, GROUP, mesh.shape["head"]), ("z", "y", "h"))
    rows = P(("z", "y", "h"), None)
    return jax.shard_map(
        per_device,
        mesh=parts,
        in_specs=(rows, rows, rows, rows, P(), P(("z", "y"), "h", None)),
        out_specs=(rows,) * 4,
        check_vma=False,
    )
```

```python
import math

import jax
import jax.numpy as jnp
from jax import lax
from jax.experimental import pallas as pl
from jax.experimental.pallas import tpu as pltpu
from jax.sharding import Mesh
from jax.sharding import PartitionSpec as P

HEADS = 32
HEAD_DIM = 128
BLOCK = 512
REACH = 3
GROUP = 4
DOCS = 16
CHUNK = 64
PER_BLOCK = BLOCK // CHUNK
NEGATIVE = -1e30
SCALE = HEAD_DIM ** (-0.5)
SCALE_LOG2 = SCALE * math.log2(math.e)
LOW = jnp.bfloat16
MIB = 1024 * 1024

NT = (((1,), (1,)), ((), ()))
NN = (((1,), (0,)), ((), ()))
VMEM = pl.BlockSpec(memory_space=pltpu.VMEM)
SMEM = pl.BlockSpec(memory_space=pltpu.SMEM)
ANY = pl.BlockSpec(memory_space=pl.ANY)


def dot(a, b, dims=NN):
    return lax.dot_general(a, b, dims, preferred_element_type=jnp.float32)


def part_of(ref, block, array):
    start = pl.multiple_of(block * PER_BLOCK, PER_BLOCK)
    rows = ref[pl.ds(start, PER_BLOCK), array * CHUNK : (array + 1) * CHUNK]
    return rows.reshape(BLOCK, HEAD_DIM)


def put_part(ref, block, array, rows):
    start = pl.multiple_of(block * PER_BLOCK, PER_BLOCK)
    rows = rows.astype(LOW).reshape(PER_BLOCK, CHUNK, HEAD_DIM)
    ref[pl.ds(start, PER_BLOCK), array * CHUNK : (array + 1) * CHUNK] = rows


def picks_of(sent, block):
    start = pl.multiple_of(block * PER_BLOCK, PER_BLOCK)
    lines = jnp.max(sent[pl.ds(start, PER_BLOCK)].astype(jnp.float32), axis=0)
    return [jnp.max(lines[i : i + 1]).astype(jnp.int32) for i in range(2)]


def rows_of(block):
    return pl.ds(pl.multiple_of(block * BLOCK, BLOCK), BLOCK)


class Marks:
    def __init__(self, docs):
        self.docs = jnp.transpose(docs[...])
        self.lane = lax.broadcasted_iota(jnp.int32, (128, 128), 1).astype(jnp.float32)

    def same(self, block):
        columns = [self.docs[:, 4 * block + i : 4 * block + i + 1] for i in range(4)]
        return [jnp.broadcast_to(c, (128, 128)) == self.lane for c in columns]

    def keys(self, block):
        return jnp.concatenate([jnp.where(s, 1.0, 0.0).astype(LOW) for s in self.same(block)], axis=0)

    def queries(self, block):
        free = self.lane > DOCS
        parts = [jnp.where(jnp.logical_or(s, free), 0.0, NEGATIVE) for s in self.same(block)]
        return jnp.concatenate(parts, axis=0).astype(LOW)


def causal_mask():
    return lax.broadcasted_iota(jnp.int32, (BLOCK, BLOCK), 0) <= lax.broadcasted_iota(
        jnp.int32, (BLOCK, BLOCK), 1
    )


def score_blocks(keys, slots, query_wide, causal):
    scores = [dot(keys[rows_of(s), :], query_wide, NT) for s in slots]
    scores[-1] = jnp.where(causal, scores[-1], NEGATIVE)
    return scores


def softmax_blocks(scores):
    top = jnp.max(scores[0], axis=0, keepdims=True)
    for s in scores[1:]:
        top = jnp.maximum(top, jnp.max(s, axis=0, keepdims=True))
    top = top * SCALE_LOG2
    probs = [jnp.exp2(s * SCALE_LOG2 - top) for s in scores]
    total = sum(jnp.sum(p, axis=0, keepdims=True) for p in probs)
    return top, total, probs


def finish_block(slots, probs, query, grad, values, keys_t, values_t, add):
    out_t = sum(dot(values_t[s], p) for s, p in zip(slots, probs))
    grad_t = jnp.transpose(grad.astype(jnp.float32))
    delta = jnp.sum(grad_t * out_t, axis=0, keepdims=True)
    query_t = 0.0
    for i, (s, p) in enumerate(zip(slots, probs)):
        prob_grad = dot(values(s), grad, NT)
        score_grad = (p.astype(jnp.float32) * (prob_grad - delta)).astype(LOW)
        query_t = query_t + dot(keys_t[s], score_grad)
        add(i, s, score_grad, p)
    return jnp.transpose(out_t), jnp.transpose(query_t * SCALE)


def last_block(sent, docs, kv, qd, od, part, picks, keys, keys_t, values_t):
    for b in range(GROUP):
        picks[2 * b], picks[2 * b + 1] = picks_of(sent, b)
    marks = Marks(docs)
    for b in range(GROUP):
        key = part_of(kv, b, 0)
        keys[pl.ds(b * BLOCK, BLOCK), :HEAD_DIM] = key
        keys[pl.ds(b * BLOCK, BLOCK), HEAD_DIM:] = marks.keys(REACH + b)
        keys_t[b] = jnp.transpose(key)
        values_t[b] = jnp.transpose(part_of(kv, b, 1))
    own = GROUP - 1
    query, grad = part_of(qd, 0, 0), part_of(qd, 0, 1)
    query_wide = jnp.concatenate([query, marks.queries(REACH + own)], axis=1)
    slots = [own - picks[2 * own], own - picks[2 * own + 1], own]
    scores = score_blocks(keys, slots, query_wide, causal_mask())
    _, total, probs = softmax_blocks(scores)
    inverse = 1.0 / total
    probs = [(p * inverse).astype(LOW) for p in probs]
    unused = own * (own - 1) // 2 - slots[0] - slots[1]
    zero = jnp.zeros((BLOCK, HEAD_DIM), LOW)
    put_part(part, unused, 0, zero)
    put_part(part, unused, 1, zero)

    def add(i, s, score_grad, p):
        put_part(part, s, 0, dot(score_grad, query) * SCALE)
        put_part(part, s, 1, dot(p, grad))

    out, query_grad = finish_block(
        slots, probs, query, grad, lambda s: part_of(kv, s, 1), keys_t, values_t, add
    )
    put_part(od, 0, 0, out)
    put_part(od, 0, 1, query_grad)


def window_slots(picks, j):
    own = REACH + j
    return [own - picks[2 * j], own - picks[2 * j + 1], own]


def totals(picks, docs, kv, key_halo, qd, stats, keys, values_t):
    marks = Marks(docs)
    for b in range(2 * REACH):
        key = part_of(kv, b - REACH, 0) if b >= REACH else key_halo[
            pl.ds(b * PER_BLOCK, PER_BLOCK)
        ].reshape(BLOCK, HEAD_DIM)
        keys[pl.ds(b * BLOCK, BLOCK), :HEAD_DIM] = key
        keys[pl.ds(b * BLOCK, BLOCK), HEAD_DIM:] = marks.keys(b)
    for b in range(REACH):
        values_t[b] = jnp.transpose(part_of(kv, b, 1))
    causal = causal_mask()
    stats[...] = jnp.zeros_like(stats)
    column = lax.broadcasted_iota(jnp.int32, (1, BLOCK), 1)
    line = jnp.zeros((1, BLOCK), jnp.int32)
    for i in range(2 * REACH):
        line = jnp.where(column == i, picks[i], line)
    stats[6:7, :] = line.astype(jnp.float32)
    for j in range(REACH):
        query, grad = part_of(qd, j, 0), part_of(qd, j, 1)
        query_wide = jnp.concatenate([query, marks.queries(REACH + j)], axis=1)
        slots = window_slots(picks, j)
        top, total, probs = softmax_blocks(score_blocks(keys, slots, query_wide, causal))
        stats[j : j + 1, :] = top + jnp.log2(total)
        local_t = dot(values_t[j], probs[-1].astype(LOW))
        if j > 0:
            for s, p in zip(slots[:-1], probs[:-1]):
                here = jnp.where(s >= REACH, 1.0, 0.0)
                local_t += here * dot(values_t[jnp.maximum(s - REACH, 0)], p.astype(LOW))
        grad_t = jnp.transpose(grad.astype(jnp.float32))
        delta = jnp.sum(grad_t * local_t, axis=0, keepdims=True)
        stats[REACH + j : REACH + j + 1, :] = delta / total


def first_blocks(
    picks, docs, kv, key_halo, value_halo, qd, stats, _, od, part,
    keys, values, keys_t, values_t, key_sum, value_sum,
):
    marks = Marks(docs)
    for b in range(2 * REACH):
        rows = pl.ds(b * BLOCK, BLOCK)
        if b < REACH:
            at = pl.ds(b * PER_BLOCK, PER_BLOCK)
            key = key_halo[at].reshape(BLOCK, HEAD_DIM)
            value = value_halo[at].reshape(BLOCK, HEAD_DIM)
        else:
            key, value = part_of(kv, b - REACH, 0), part_of(kv, b - REACH, 1)
        keys[rows, :HEAD_DIM] = key
        keys[rows, HEAD_DIM:] = marks.keys(b)
        values[rows, :] = value
        keys_t[b] = jnp.transpose(key)
        values_t[b] = jnp.transpose(value)
    key_sum[...] = jnp.zeros_like(key_sum)
    value_sum[...] = jnp.zeros_like(value_sum)
    causal = causal_mask()
    for j in range(REACH):
        query, grad = part_of(qd, j, 0), part_of(qd, j, 1)
        query_wide = jnp.concatenate([query, marks.queries(REACH + j)], axis=1)
        slots = window_slots(picks, j)
        log_total = stats[j : j + 1, :]
        scores = score_blocks(keys, slots, query_wide, causal)
        probs = [jnp.exp2(s * SCALE_LOG2 - log_total).astype(LOW) for s in scores]

        def add(i, s, score_grad, p):
            if j == 0 and i < 2:
                return
            key_sum[rows_of(s), :] += dot(score_grad, query)
            value_sum[rows_of(s), :] += dot(p, grad)

        out, query_grad = finish_block(
            slots, probs, query, grad, lambda s: values[rows_of(s), :], keys_t, values_t, add
        )
        put_part(od, j, 0, out)
        put_part(od, j, 1, query_grad)
    for b in range(REACH):
        rows = pl.ds((REACH + b) * BLOCK, BLOCK)
        put_part(part, b, 0, key_sum[rows, :] * SCALE)
        put_part(part, b, 1, value_sum[rows, :])


def later_queries(
    picks, docs, kv, qd_next, stats, last_part, first_part, _, dkv, keys, key_sum, value_sum
):
    marks = Marks(docs)
    for b in range(1, GROUP):
        rows = pl.ds((b - 1) * BLOCK, BLOCK)
        keys[rows, :HEAD_DIM] = part_of(kv, b, 0)
        keys[rows, HEAD_DIM:] = marks.keys(REACH + b)
    key_sum[...] = jnp.zeros_like(key_sum)
    value_sum[...] = jnp.zeros_like(value_sum)
    for j in range(REACH):
        query, grad = part_of(qd_next, j, 0), part_of(qd_next, j, 1)
        query_wide = jnp.concatenate([query, marks.queries(REACH + GROUP + j)], axis=1)
        log_total = stats[j : j + 1, :]
        delta = stats[REACH + j : REACH + j + 1, :]
        first, second = [jnp.maximum(picks[6, 2 * j + i].astype(jnp.int32), 1) for i in range(2)]
        if j == 0:
            chosen = [(GROUP - first, log_total), (GROUP - second, log_total)]
        else:
            chosen = []
            for offset in range(j + 1, REACH + 1):
                used = jnp.logical_or(first == offset, second == offset)
                chosen.append((GROUP + j - offset, jnp.where(used, log_total, -NEGATIVE)))
        probs, products = [], []
        for b, shift in chosen:
            scores = dot(keys[rows_of(b - 1), :], query_wide, NT)
            p = jnp.exp2(scores * SCALE_LOG2 - shift)
            product = p * dot(part_of(kv, b, 1), grad, NT)
            delta = delta + jnp.sum(product, axis=0, keepdims=True)
            probs.append(p)
            products.append(product)
        for (b, _), p, product in zip(chosen, probs, products):
            score_grad = (product - p * delta).astype(LOW)
            key_sum[rows_of(b - 1), :] += dot(score_grad, query)
            value_sum[rows_of(b - 1), :] += dot(p.astype(LOW), grad)
    for b in range(GROUP):
        for array, ref, scale in ((0, key_sum, SCALE), (1, value_sum, 1.0)):
            total = part_of(last_part, b, array).astype(jnp.float32)
            if b < REACH:
                total = total + part_of(first_part, b, array).astype(jnp.float32)
            if b > 0:
                total = total + ref[pl.ds((b - 1) * BLOCK, BLOCK), :] * scale
            put_part(dkv, b, array, total)


def block_spec(shape, index):
    return pl.BlockSpec(shape, lambda *_: index)


def params(mib):
    return pltpu.CompilerParams(vmem_limit_bytes=mib * MIB)


def cost(pairs, products, mib):
    area = pairs * BLOCK * BLOCK
    return pl.CostEstimate(
        flops=2 * products * area * HEAD_DIM, bytes_accessed=mib * MIB, transcendentals=area
    )


def chunks(count, arrays):
    return (count, arrays * CHUNK, HEAD_DIM)


def array(shape, dtype=LOW):
    return jax.ShapeDtypeStruct(shape, dtype)


KV_SPEC = block_spec(chunks(HEADS, 2), (0, 0, 0))
FIRST = REACH * PER_BLOCK


def run_last(docs, x):
    wide, high = 2 * HEAD_DIM, GROUP * BLOCK
    return pl.pallas_call(
        last_block,
        grid=(1,),
        out_shape=(
            array(chunks(HEADS, 4)),
            array(chunks(HEADS, 2)),
            array((2 * GROUP,), jnp.int32),
        ),
        in_specs=[
            block_spec((HEADS, 16, HEAD_DIM), (0, 16, 0)),
            VMEM,
            KV_SPEC,
            block_spec(chunks(PER_BLOCK, 2), (REACH, 1, 0)),
        ],
        out_specs=(block_spec(chunks(PER_BLOCK, 2), (REACH, 0, 0)), KV_SPEC, SMEM),
        scratch_shapes=[
            pltpu.VMEM((high, wide), LOW),
            pltpu.VMEM((GROUP, HEAD_DIM, BLOCK), LOW),
            pltpu.VMEM((GROUP, HEAD_DIM, BLOCK), LOW),
        ],
        compiler_params=params(24),
        cost_estimate=cost(3, 6, 3),
        name="last_block",
    )(x, docs, x, x)


def run_totals(picks, docs, x, key_halo):
    wide, high = 2 * HEAD_DIM, 2 * REACH * BLOCK
    return pl.pallas_call(
        totals,
        grid=(1,),
        out_shape=array((8, BLOCK), jnp.float32),
        in_specs=[
            SMEM,
            VMEM,
            block_spec(chunks(FIRST, 2), (0, 0, 0)),
            VMEM,
            block_spec(chunks(FIRST, 2), (0, 1, 0)),
        ],
        out_specs=VMEM,
        scratch_shapes=[
            pltpu.VMEM((high, wide), LOW),
            pltpu.VMEM((REACH, HEAD_DIM, BLOCK), LOW),
        ],
        compiler_params=params(24),
        cost_estimate=cost(9, 2, 2),
        name="totals",
    )(picks, docs, x, key_halo, x)


def run_first(picks, docs, x, key_halo, value_halo, stats, y):
    wide, high = 2 * HEAD_DIM, 2 * REACH * BLOCK
    return pl.pallas_call(
        first_blocks,
        grid=(1,),
        out_shape=(array(y.shape), array(chunks(FIRST, 2))),
        in_specs=[
            SMEM,
            VMEM,
            block_spec(chunks(FIRST, 2), (0, 0, 0)),
            VMEM,
            VMEM,
            block_spec(chunks(FIRST, 2), (0, 1, 0)),
            VMEM,
            ANY,
        ],
        out_specs=(block_spec(chunks(FIRST, 2), (0, 0, 0)), VMEM),
        scratch_shapes=[
            pltpu.VMEM((high, wide), LOW),
            pltpu.VMEM((high, HEAD_DIM), LOW),
            pltpu.VMEM((2 * REACH, HEAD_DIM, BLOCK), LOW),
            pltpu.VMEM((2 * REACH, HEAD_DIM, BLOCK), LOW),
            pltpu.VMEM((high, HEAD_DIM), jnp.float32),
            pltpu.VMEM((high, HEAD_DIM), jnp.float32),
        ],
        input_output_aliases={7: 0},
        compiler_params=params(32),
        cost_estimate=cost(9, 6, 5),
        name="first_blocks",
    )(picks, docs, x, key_halo, value_halo, x, stats, y)


def run_later(docs, x, qd_next, stats, last_part, first_part, y):
    wide, high = 2 * HEAD_DIM, REACH * BLOCK
    qd_spec = block_spec(chunks(FIRST, 2), (0, 0, 0))
    return pl.pallas_call(
        later_queries,
        grid=(1,),
        out_shape=array(y.shape),
        in_specs=[SMEM, VMEM, KV_SPEC, qd_spec, VMEM, VMEM, VMEM, ANY],
        out_specs=block_spec(chunks(HEADS, 2), (0, 1, 0)),
        scratch_shapes=[
            pltpu.VMEM((high, wide), LOW),
            pltpu.VMEM((high, HEAD_DIM), jnp.float32),
            pltpu.VMEM((high, HEAD_DIM), jnp.float32),
        ],
        input_output_aliases={7: 0},
        compiler_params=params(24),
        cost_estimate=cost(5, 4, 5),
        name="later_queries",
    )(stats, docs, x, qd_next, stats, last_part, first_part, y)


STEPS = 2
STEP_H = PER_BLOCK // STEPS
SENT = 4 * CHUNK + 16


def pack(picks, *args):
    *rows, packed = args
    line = lax.broadcasted_iota(jnp.int32, (16, HEAD_DIM), 0)
    mine = lax.axis_index("h") - pl.program_id(0) * STEP_H
    for k in range(GROUP):
        pair = jnp.where(line == 0, picks[0, 0, k], picks[0, 1, k]).astype(jnp.float32)
        for h in range(STEP_H):
            packed[k, h, 4 * CHUNK :] = jnp.where(mine == h, pair, 0.0).astype(LOW)
            start = (h * GROUP + k) * HEAD_DIM
            for i, ref in enumerate(rows):
                packed[k, h, i * CHUNK : (i + 1) * CHUNK] = ref[:, start : start + HEAD_DIM]


def unpack(packed, *rows):
    for k in range(GROUP):
        for h in range(STEP_H):
            start = (h * GROUP + k) * HEAD_DIM
            for i, ref in enumerate(rows):
                ref[:, start : start + HEAD_DIM] = packed[k, h, i * CHUNK : (i + 1) * CHUNK]


def packed_spec(rows):
    return pl.BlockSpec((GROUP, STEP_H, rows, HEAD_DIM), lambda i: (0, i, 0, 0))


ROWS = pl.BlockSpec((CHUNK, STEP_H * GROUP * HEAD_DIM), lambda i: (0, i))


def run_pack(picks, *rows):
    packed = pl.pallas_call(
        pack,
        grid=(STEPS,),
        out_shape=array((GROUP, PER_BLOCK, SENT, HEAD_DIM)),
        in_specs=[SMEM] + [ROWS] * 4,
        out_specs=packed_spec(SENT),
        cost_estimate=cost(0, 0, 4),
        name="pack",
    )(picks, *rows)
    return packed.reshape(HEADS, SENT, HEAD_DIM)


def run_unpack(packed):
    return pl.pallas_call(
        unpack,
        grid=(STEPS,),
        out_shape=(array((CHUNK, HEADS * HEAD_DIM)),) * 4,
        in_specs=[packed_spec(4 * CHUNK)],
        out_specs=(ROWS,) * 4,
        cost_estimate=cost(0, 0, 4),
        name="unpack",
    )(packed.reshape(GROUP, PER_BLOCK, 4 * CHUNK, HEAD_DIM))


def per_device(queries, key_rows, value_rows, out_grad, doc_ids, picks):
    plane = lax.axis_index("z")
    planes = lax.axis_size("z")
    forward = [(i, i + 1) for i in range(planes - 1)]
    backward = [(i + 1, i) for i in range(planes - 1)]

    def exchange(packed):
        return lax.all_to_all(packed, ("y", "h"), split_axis=0, concat_axis=0)

    x = exchange(run_pack(jnp.swapaxes(picks, 1, 2), key_rows, value_rows, queries, out_grad))

    edge = jnp.full((REACH * BLOCK,), DOCS, jnp.int32)
    docs = jnp.concatenate([edge, doc_ids, edge])
    docs = lax.dynamic_slice_in_dim(
        docs, plane * (GROUP * BLOCK), (2 * REACH + GROUP) * BLOCK, 0
    )
    docs = docs.astype(jnp.float32).reshape(-1, HEAD_DIM)

    key_halo = lax.ppermute(x[PER_BLOCK:, :CHUNK], "z", forward)
    value_halo = lax.ppermute(x[PER_BLOCK:, CHUNK : 2 * CHUNK], "z", forward)
    qd_next = lax.ppermute(x[:FIRST, 2 * CHUNK : 4 * CHUNK], "z", backward)

    y, last_part, picks_here = run_last(docs, x)
    stats = run_totals(picks_here, docs, x, key_halo)
    stats_next = lax.ppermute(stats, "z", backward)
    y, first_part = run_first(picks_here, docs, x, key_halo, value_halo, stats, y)
    y = run_later(docs, x, qd_next, stats_next, last_part, first_part, y)
    return tuple(run_unpack(exchange(y)))


def solution(mesh):
    planes = mesh.shape["seq"] // GROUP
    parts = Mesh(mesh.devices.reshape(planes, GROUP, mesh.shape["head"]), ("z", "y", "h"))
    rows = P(("z", "y", "h"), None)
    return jax.shard_map(
        per_device,
        mesh=parts,
        in_specs=(rows, rows, rows, rows, P(), P(("z", "y"), "h", None)),
        out_specs=(rows,) * 4,
        check_vma=False,
    )
```

```python
import math

import jax
import jax.numpy as jnp
from jax import lax
from jax.experimental import pallas as pl
from jax.experimental.pallas import tpu as pltpu
from jax.sharding import Mesh
from jax.sharding import PartitionSpec as P

HEADS = 32
HEAD_DIM = 128
BLOCK = 512
REACH = 3
GROUP = 4
DOCS = 16
CHUNK = 64
PER_BLOCK = BLOCK // CHUNK
NEGATIVE = -1e30
SCALE = HEAD_DIM ** (-0.5)
SCALE_LOG2 = SCALE * math.log2(math.e)
LOW = jnp.bfloat16
MIB = 1024 * 1024

NT = (((1,), (1,)), ((), ()))
NN = (((1,), (0,)), ((), ()))
VMEM = pl.BlockSpec(memory_space=pltpu.VMEM)
SMEM = pl.BlockSpec(memory_space=pltpu.SMEM)


def dot(a, b, dims=NN):
    return lax.dot_general(a, b, dims, preferred_element_type=jnp.float32)


def part_of(ref, block, array):
    start = pl.multiple_of(block * PER_BLOCK, PER_BLOCK)
    rows = ref[pl.ds(start, PER_BLOCK), array * CHUNK : (array + 1) * CHUNK]
    return rows.reshape(BLOCK, HEAD_DIM)


def put_part(ref, block, array, rows):
    start = pl.multiple_of(block * PER_BLOCK, PER_BLOCK)
    rows = rows.astype(LOW).reshape(PER_BLOCK, CHUNK, HEAD_DIM)
    ref[pl.ds(start, PER_BLOCK), array * CHUNK : (array + 1) * CHUNK] = rows


def rows_of(block):
    return pl.ds(pl.multiple_of(block * BLOCK, BLOCK), BLOCK)


class Marks:
    def __init__(self, docs):
        self.rows = docs
        self.docs = jnp.transpose(docs[...])
        self.lane = lax.broadcasted_iota(jnp.int32, (128, 128), 1).astype(jnp.float32)

    def same(self, block):
        columns = [self.docs[:, 4 * block + i : 4 * block + i + 1] for i in range(4)]
        return [jnp.broadcast_to(c, (128, 128)) == self.lane for c in columns]

    def keys(self, block):
        return jnp.concatenate([jnp.where(s, 1.0, 0.0).astype(LOW) for s in self.same(block)], axis=0)

    def wide_t(self, query, block):
        rows = [self.rows[4 * block + i : 4 * block + i + 1, :] for i in range(4)]
        docs = jnp.broadcast_to(jnp.concatenate(rows, axis=1), (HEAD_DIM, BLOCK))
        column = lax.broadcasted_iota(jnp.int32, (HEAD_DIM, BLOCK), 0).astype(jnp.float32)
        free = jnp.logical_or(docs == column, column > DOCS)
        extra = jnp.where(free, 0.0, NEGATIVE).astype(LOW)
        return jnp.concatenate([jnp.transpose(query), extra], axis=0)


def causal_mask():
    return lax.broadcasted_iota(jnp.int32, (BLOCK, BLOCK), 0) <= lax.broadcasted_iota(
        jnp.int32, (BLOCK, BLOCK), 1
    )


def score_blocks(keys, slots, query_wide, causal):
    scores = [dot(keys[rows_of(s), :], query_wide) for s in slots]
    scores[-1] = jnp.where(causal, scores[-1], NEGATIVE)
    return scores


def softmax_blocks(scores):
    top = jnp.max(scores[0], axis=0, keepdims=True)
    for s in scores[1:]:
        top = jnp.maximum(top, jnp.max(s, axis=0, keepdims=True))
    top = top * SCALE_LOG2
    probs = [jnp.exp2(s * SCALE_LOG2 - top) for s in scores]
    total = sum(jnp.sum(p, axis=0, keepdims=True) for p in probs)
    return top, total, probs


def finish_block(slots, probs, query, grad, values, keys_t, values_t, add):
    out_t = sum(dot(values_t[s], p) for s, p in zip(slots, probs))
    grad_t = jnp.transpose(grad)
    delta = jnp.sum(grad_t.astype(jnp.float32) * out_t, axis=0, keepdims=True)
    query_t = 0.0
    for i, (s, p) in enumerate(zip(slots, probs)):
        prob_grad = dot(values(s), grad_t)
        score_grad = (p.astype(jnp.float32) * (prob_grad - delta)).astype(LOW)
        query_t = query_t + dot(keys_t[s], score_grad)
        add(i, s, score_grad, p)
    return jnp.transpose(out_t), jnp.transpose(query_t * SCALE)


def halos(x, key_halo, value_halo, qd_halo):
    key_halo[...] = x[PER_BLOCK:, :CHUNK]
    value_halo[...] = x[PER_BLOCK:, CHUNK : 2 * CHUNK]
    qd_halo[...] = x[:FIRST, 2 * CHUNK : 4 * CHUNK]


def last_block(docs, x, od, part, picks, keys, keys_t, values_t):
    for b in range(GROUP):
        sent = x[b * PER_BLOCK : (b + 1) * PER_BLOCK, 4 * CHUNK :].astype(jnp.float32)
        lines = jnp.max(sent, axis=0)
        for i in range(2):
            picks[2 * b + i] = jnp.max(lines[i : i + 1]).astype(jnp.int32)
    marks = Marks(docs)
    for b in range(GROUP):
        key = part_of(x, b, 0)
        keys[pl.ds(b * BLOCK, BLOCK), :HEAD_DIM] = key
        keys[pl.ds(b * BLOCK, BLOCK), HEAD_DIM:] = marks.keys(REACH + b)
        keys_t[b] = jnp.transpose(key)
        values_t[b] = jnp.transpose(part_of(x, b, 1))
    own = GROUP - 1
    query, grad = part_of(x, own, 2), part_of(x, own, 3)
    query_wide = marks.wide_t(query, REACH + own)
    slots = [own - picks[2 * own], own - picks[2 * own + 1], own]
    scores = score_blocks(keys, slots, query_wide, causal_mask())
    _, total, probs = softmax_blocks(scores)
    inverse = 1.0 / total
    probs = [(p * inverse).astype(LOW) for p in probs]
    unused = own * (own - 1) // 2 - slots[0] - slots[1]
    zero = jnp.zeros((BLOCK, HEAD_DIM), LOW)
    put_part(part, unused, 0, zero)
    put_part(part, unused, 1, zero)

    def add(i, s, score_grad, p):
        put_part(part, s, 0, dot(score_grad, query) * SCALE)
        put_part(part, s, 1, dot(p, grad))

    out, query_grad = finish_block(
        slots, probs, query, grad, lambda s: part_of(x, s, 1), keys_t, values_t, add
    )
    put_part(od, 0, 0, out)
    put_part(od, 0, 1, query_grad)


def window_slots(picks, j):
    own = REACH + j
    return [own - picks[2 * j], own - picks[2 * j + 1], own]


def totals(picks, docs, x, key_halo, stats, probs_out, keys, values_t):
    marks = Marks(docs)
    for b in range(2 * REACH):
        key = part_of(x, b - REACH, 0) if b >= REACH else key_halo[
            pl.ds(b * PER_BLOCK, PER_BLOCK)
        ].reshape(BLOCK, HEAD_DIM)
        keys[pl.ds(b * BLOCK, BLOCK), :HEAD_DIM] = key
        keys[pl.ds(b * BLOCK, BLOCK), HEAD_DIM:] = marks.keys(b)
    for b in range(REACH):
        values_t[b] = jnp.transpose(part_of(x, b, 1))
    causal = causal_mask()
    stats[...] = jnp.zeros_like(stats)
    column = lax.broadcasted_iota(jnp.int32, (1, BLOCK), 1)
    line = jnp.zeros((1, BLOCK), jnp.int32)
    for i in range(2 * REACH):
        line = jnp.where(column == i, picks[i], line)
    stats[6:7, :] = line.astype(jnp.float32)
    def scores_of(j):
        query_wide = marks.wide_t(part_of(x, j, 2), REACH + j)
        slots = window_slots(picks, j)
        return slots, score_blocks(keys, slots, query_wide, causal)

    ahead = scores_of(0)
    for j in range(REACH):
        slots, scores = ahead
        if j + 1 < REACH:
            ahead = scores_of(j + 1)
        top, total, probs = softmax_blocks(scores)
        probs = [p.astype(LOW) for p in probs]
        for i, p in enumerate(probs):
            probs_out[3 * j + i] = p
        stats[j : j + 1, :] = top + jnp.log2(total)
        stats[8 + j : 9 + j, :] = 1.0 / total
        local_t = dot(values_t[j], probs[-1])
        if j > 0:
            for s, p in zip(slots[:-1], probs[:-1]):
                here = jnp.where(s >= REACH, 1.0, 0.0)
                local_t += here * dot(values_t[jnp.maximum(s - REACH, 0)], p)
        grad_t = jnp.transpose(part_of(x, j, 3))
        delta = jnp.sum(grad_t.astype(jnp.float32) * local_t, axis=0, keepdims=True)
        stats[REACH + j : REACH + j + 1, :] = delta / total


def first_blocks(
    picks, x, key_halo, value_halo, stats, probs_in, od, part,
    keys, values, keys_t, values_t, key_sum, value_sum,
):
    for b in range(2 * REACH):
        rows = pl.ds(b * BLOCK, BLOCK)
        if b < REACH:
            at = pl.ds(b * PER_BLOCK, PER_BLOCK)
            key = key_halo[at].reshape(BLOCK, HEAD_DIM)
            value = value_halo[at].reshape(BLOCK, HEAD_DIM)
        else:
            key, value = part_of(x, b - REACH, 0), part_of(x, b - REACH, 1)
        keys[rows, :] = key
        values[rows, :] = value
        keys_t[b] = jnp.transpose(key)
        values_t[b] = jnp.transpose(value)
    key_sum[...] = jnp.zeros_like(key_sum)
    value_sum[...] = jnp.zeros_like(value_sum)
    for j in range(REACH):
        query, grad = part_of(x, j, 2), part_of(x, j, 3)
        slots = window_slots(picks, j)
        inverse = stats[8 + j : 9 + j, :]
        probs = [(probs_in[3 * j + i].astype(jnp.float32) * inverse).astype(LOW) for i in range(3)]

        def add(i, s, score_grad, p):
            if j == 0 and i < 2:
                return
            key_sum[rows_of(s), :] += dot(score_grad, query)
            value_sum[rows_of(s), :] += dot(p, grad)

        out, query_grad = finish_block(
            slots, probs, query, grad, lambda s: values[rows_of(s), :], keys_t, values_t, add
        )
        put_part(od, j, 0, out)
        put_part(od, j, 1, query_grad)
    for b in range(REACH):
        rows = pl.ds((REACH + b) * BLOCK, BLOCK)
        put_part(part, b, 0, key_sum[rows, :] * SCALE)
        put_part(part, b, 1, value_sum[rows, :])


def later_queries(
    picks, docs, x, qd_next, stats, last_od, last_part, first_od, first_part, y,
    keys, key_sum, value_sum,
):
    y[:FIRST, : 2 * CHUNK] = first_od[...]
    y[FIRST:, : 2 * CHUNK] = last_od[...]
    marks = Marks(docs)
    for b in range(1, GROUP):
        rows = pl.ds((b - 1) * BLOCK, BLOCK)
        keys[rows, :HEAD_DIM] = part_of(x, b, 0)
        keys[rows, HEAD_DIM:] = marks.keys(REACH + b)
    key_sum[...] = jnp.zeros_like(key_sum)
    value_sum[...] = jnp.zeros_like(value_sum)
    for j in range(REACH):
        query, grad = part_of(qd_next, j, 0), part_of(qd_next, j, 1)
        query_wide = marks.wide_t(query, REACH + GROUP + j)
        log_total = stats[j : j + 1, :]
        delta = stats[REACH + j : REACH + j + 1, :]
        first, second = [jnp.maximum(picks[6, 2 * j + i].astype(jnp.int32), 1) for i in range(2)]
        if j == 0:
            chosen = [(GROUP - first, log_total), (GROUP - second, log_total)]
        else:
            chosen = []
            for offset in range(j + 1, REACH + 1):
                used = jnp.logical_or(first == offset, second == offset)
                chosen.append((GROUP + j - offset, jnp.where(used, log_total, -NEGATIVE)))
        grad_t = jnp.transpose(grad)
        probs, products = [], []
        for b, shift in chosen:
            scores = dot(keys[rows_of(b - 1), :], query_wide)
            p = jnp.exp2(scores * SCALE_LOG2 - shift)
            product = p * dot(part_of(x, b, 1), grad_t)
            delta = delta + jnp.sum(product, axis=0, keepdims=True)
            probs.append(p)
            products.append(product)
        for (b, _), p, product in zip(chosen, probs, products):
            score_grad = (product - p * delta).astype(LOW)
            key_sum[rows_of(b - 1), :] += dot(score_grad, query)
            value_sum[rows_of(b - 1), :] += dot(p.astype(LOW), grad)
    for b in range(GROUP):
        for array, ref, scale in ((0, key_sum, SCALE), (1, value_sum, 1.0)):
            total = part_of(last_part, b, array).astype(jnp.float32)
            if b < REACH:
                total = total + part_of(first_part, b, array).astype(jnp.float32)
            if b > 0:
                total = total + ref[pl.ds((b - 1) * BLOCK, BLOCK), :] * scale
            put_part(y, b, 2 + array, total)


def params(mib):
    return pltpu.CompilerParams(vmem_limit_bytes=mib * MIB)


def cost(pairs, products, mib):
    area = pairs * BLOCK * BLOCK
    return pl.CostEstimate(
        flops=2 * products * area * HEAD_DIM, bytes_accessed=mib * MIB, transcendentals=area
    )


def chunks(count, arrays):
    return (count, arrays * CHUNK, HEAD_DIM)


def array(shape, dtype=LOW):
    return jax.ShapeDtypeStruct(shape, dtype)


FIRST = REACH * PER_BLOCK


def run_halos(x):
    one, two = array((FIRST, CHUNK, HEAD_DIM)), array(chunks(FIRST, 2))
    return pl.pallas_call(
        halos,
        out_shape=(one, one, two),
        in_specs=[VMEM],
        out_specs=(VMEM,) * 3,
        compiler_params=params(8),
        cost_estimate=cost(0, 0, 3),
        name="halos",
    )(x)


def run_last(docs, x):
    wide, high = 2 * HEAD_DIM, GROUP * BLOCK
    return pl.pallas_call(
        last_block,
        out_shape=(
            array(chunks(PER_BLOCK, 2)),
            array(chunks(HEADS, 2)),
            array((2 * GROUP,), jnp.int32),
        ),
        in_specs=[VMEM, VMEM],
        out_specs=(VMEM, VMEM, SMEM),
        scratch_shapes=[
            pltpu.VMEM((high, wide), LOW),
            pltpu.VMEM((GROUP, HEAD_DIM, BLOCK), LOW),
            pltpu.VMEM((GROUP, HEAD_DIM, BLOCK), LOW),
        ],
        compiler_params=params(24),
        cost_estimate=cost(3, 6, 3),
        name="last_block",
    )(docs, x)


def run_totals(picks, docs, x, key_halo):
    wide, high = 2 * HEAD_DIM, 2 * REACH * BLOCK
    return pl.pallas_call(
        totals,
        out_shape=(array((16, BLOCK), jnp.float32), array((3 * REACH, BLOCK, BLOCK))),
        in_specs=[SMEM, VMEM, VMEM, VMEM],
        out_specs=(VMEM, VMEM),
        scratch_shapes=[
            pltpu.VMEM((high, wide), LOW),
            pltpu.VMEM((REACH, HEAD_DIM, BLOCK), LOW),
        ],
        compiler_params=params(24),
        cost_estimate=cost(9, 2, 2),
        name="totals",
    )(picks, docs, x, key_halo)


def run_first(picks, x, key_halo, value_halo, stats, probs):
    high = 2 * REACH * BLOCK
    return pl.pallas_call(
        first_blocks,
        out_shape=(array(chunks(FIRST, 2)),) * 2,
        in_specs=[SMEM] + [VMEM] * 5,
        out_specs=(VMEM, VMEM),
        scratch_shapes=[
            pltpu.VMEM((high, HEAD_DIM), LOW),
            pltpu.VMEM((high, HEAD_DIM), LOW),
            pltpu.VMEM((2 * REACH, HEAD_DIM, BLOCK), LOW),
            pltpu.VMEM((2 * REACH, HEAD_DIM, BLOCK), LOW),
            pltpu.VMEM((high, HEAD_DIM), jnp.float32),
            pltpu.VMEM((high, HEAD_DIM), jnp.float32),
        ],
        compiler_params=params(32),
        cost_estimate=cost(9, 6, 5),
        name="first_blocks",
    )(picks, x, key_halo, value_halo, stats, probs)


def run_later(docs, x, qd_next, stats, *parts):
    wide, high = 2 * HEAD_DIM, REACH * BLOCK
    return pl.pallas_call(
        later_queries,
        out_shape=array(chunks(HEADS, 4)),
        in_specs=[SMEM] + [VMEM] * 8,
        out_specs=VMEM,
        scratch_shapes=[
            pltpu.VMEM((high, wide), LOW),
            pltpu.VMEM((high, HEAD_DIM), jnp.float32),
            pltpu.VMEM((high, HEAD_DIM), jnp.float32),
        ],
        compiler_params=params(24),
        cost_estimate=cost(5, 4, 5),
        name="later_queries",
    )(stats, docs, x, qd_next, stats, *parts)


SENT = 4 * CHUNK + 16


def pack(picks_sent, k_rows, v_rows, q_rows, d_rows, packed, rows, done, picks, picks_done):
    sources = (k_rows, v_rows, q_rows, d_rows)
    copies = [pltpu.make_async_copy(r, rows.at[i], done.at[i]) for i, r in enumerate(sources)]
    picks_copy = pltpu.make_async_copy(picks_sent, picks, picks_done)
    for copy in copies + [picks_copy]:
        copy.start()
    picks_copy.wait()
    line = lax.broadcasted_iota(jnp.int32, (16, HEAD_DIM), 0)
    mine = lax.axis_index("h")
    for k in range(GROUP):
        pair = jnp.where(line == 0, picks[0, 0, k], picks[0, 1, k]).astype(jnp.float32)
        for h in range(PER_BLOCK):
            packed[k, h, 4 * CHUNK :] = jnp.where(mine == h, pair, 0.0).astype(LOW)
    for i, copy in enumerate(copies):
        copy.wait()
        for k in range(GROUP):
            for h in range(PER_BLOCK):
                start = (h * GROUP + k) * HEAD_DIM
                packed[k, h, i * CHUNK : (i + 1) * CHUNK] = rows[i, :, start : start + HEAD_DIM]


def unpack(packed, out, q_rows, k_rows, v_rows, rows, done):
    copies = []
    for i, target in enumerate((out, q_rows, k_rows, v_rows)):
        for k in range(GROUP):
            for h in range(PER_BLOCK):
                start = (h * GROUP + k) * HEAD_DIM
                rows[i, :, start : start + HEAD_DIM] = packed[k, h, i * CHUNK : (i + 1) * CHUNK]
        copies.append(pltpu.make_async_copy(rows.at[i], target, done.at[i]))
        copies[-1].start()
    for copy in copies:
        copy.wait()


HBM = pl.BlockSpec(memory_space=pltpu.HBM)
STAGING = [pltpu.VMEM((4, CHUNK, HEADS * HEAD_DIM), LOW), pltpu.SemaphoreType.DMA((4,))]


def run_pack(picks, *rows):
    packed = pl.pallas_call(
        pack,
        out_shape=array((GROUP, PER_BLOCK, SENT, HEAD_DIM)),
        in_specs=[HBM] * 5,
        out_specs=VMEM,
        scratch_shapes=STAGING
        + [pltpu.SMEM((1, 2, GROUP), jnp.int32), pltpu.SemaphoreType.DMA],
        compiler_params=params(16),
        cost_estimate=cost(0, 0, 4),
        name="pack",
    )(*[pltpu.with_memory_space_constraint(r, pltpu.HBM) for r in (picks, *rows)])
    return packed.reshape(HEADS, SENT, HEAD_DIM)


def run_unpack(packed):
    return pl.pallas_call(
        unpack,
        out_shape=(array((CHUNK, HEADS * HEAD_DIM)),) * 4,
        in_specs=[VMEM],
        out_specs=(HBM,) * 4,
        scratch_shapes=STAGING,
        compiler_params=params(16),
        cost_estimate=cost(0, 0, 4),
        name="unpack",
    )(packed.reshape(GROUP, PER_BLOCK, 4 * CHUNK, HEAD_DIM))


def per_device(queries, key_rows, value_rows, out_grad, doc_ids, picks):
    plane = lax.axis_index("z")
    planes = lax.axis_size("z")
    forward = [(i, i + 1) for i in range(planes - 1)]
    backward = [(i + 1, i) for i in range(planes - 1)]

    def exchange(packed):
        return lax.all_to_all(packed, ("y", "h"), split_axis=0, concat_axis=0)

    x = exchange(run_pack(jnp.swapaxes(picks, 1, 2), key_rows, value_rows, queries, out_grad))

    edge = jnp.full((REACH * BLOCK,), DOCS, jnp.int32)
    docs = jnp.concatenate([edge, doc_ids, edge])
    docs = lax.dynamic_slice_in_dim(
        docs, plane * (GROUP * BLOCK), (2 * REACH + GROUP) * BLOCK, 0
    )
    docs = docs.astype(jnp.float32).reshape(-1, HEAD_DIM)

    key_halo, value_halo, qd_next = run_halos(x)
    key_halo = lax.ppermute(key_halo, "z", forward)
    value_halo = lax.ppermute(value_halo, "z", forward)
    qd_next = lax.ppermute(qd_next, "z", backward)

    *last, picks_here = run_last(docs, x)
    stats, probs = run_totals(picks_here, docs, x, key_halo)
    stats_next = lax.ppermute(stats[:8], "z", backward)
    first = run_first(picks_here, x, key_halo, value_halo, stats, probs)
    y = run_later(docs, x, qd_next, stats_next, *last, *first)
    return tuple(run_unpack(exchange(y)))


def solution(mesh):
    planes = mesh.shape["seq"] // GROUP
    parts = Mesh(mesh.devices.reshape(planes, GROUP, mesh.shape["head"]), ("z", "y", "h"))
    rows = P(("z", "y", "h"), None)
    return jax.shard_map(
        per_device,
        mesh=parts,
        in_specs=(rows, rows, rows, rows, P(), P(("z", "y"), "h", None)),
        out_specs=(rows,) * 4,
        check_vma=False,
    )
```

```python
import math

import jax
import jax.numpy as jnp
from jax import lax
from jax.experimental import pallas as pl
from jax.experimental.pallas import tpu as pltpu
from jax.sharding import Mesh
from jax.sharding import PartitionSpec as P

HEADS = 32
HEAD_DIM = 128
BLOCK = 512
REACH = 3
GROUP = 4
DOCS = 16
CHUNK = 64
PER_BLOCK = BLOCK // CHUNK
NEGATIVE = -1e30
SCALE = HEAD_DIM ** (-0.5)
SCALE_LOG2 = SCALE * math.log2(math.e)
LOW = jnp.bfloat16
MIB = 1024 * 1024

NT = (((1,), (1,)), ((), ()))
NN = (((1,), (0,)), ((), ()))
VMEM = pl.BlockSpec(memory_space=pltpu.VMEM)
SMEM = pl.BlockSpec(memory_space=pltpu.SMEM)


def dot(a, b, dims=NN):
    return lax.dot_general(a, b, dims, preferred_element_type=jnp.float32)


def part_of(ref, block, array):
    start = pl.multiple_of(block * PER_BLOCK, PER_BLOCK)
    rows = ref[pl.ds(start, PER_BLOCK), array * CHUNK : (array + 1) * CHUNK]
    return rows.reshape(BLOCK, HEAD_DIM)


def put_part(ref, block, array, rows, first=0):
    start = pl.multiple_of(block * PER_BLOCK, PER_BLOCK) + first // CHUNK
    count = rows.shape[0] // CHUNK
    rows = rows.astype(LOW).reshape(count, CHUNK, HEAD_DIM)
    ref[pl.ds(start, count), array * CHUNK : (array + 1) * CHUNK] = rows


def rows_of(block):
    return pl.ds(pl.multiple_of(block * BLOCK, BLOCK), BLOCK)


class Marks:
    def __init__(self, docs):
        self.rows = docs
        self.docs = jnp.transpose(docs[...])
        self.lane = lax.broadcasted_iota(jnp.int32, (128, 128), 1).astype(jnp.float32)

    def same(self, block):
        columns = [self.docs[:, 4 * block + i : 4 * block + i + 1] for i in range(4)]
        return [jnp.broadcast_to(c, (128, 128)) == self.lane for c in columns]

    def keys(self, block):
        return jnp.concatenate([jnp.where(s, 1.0, 0.0).astype(LOW) for s in self.same(block)], axis=0)

    def wide_t(self, query, block):
        rows = [self.rows[4 * block + i : 4 * block + i + 1, :] for i in range(4)]
        docs = jnp.broadcast_to(jnp.concatenate(rows, axis=1), (HEAD_DIM, BLOCK))
        column = lax.broadcasted_iota(jnp.int32, (HEAD_DIM, BLOCK), 0).astype(jnp.float32)
        free = jnp.logical_or(docs == column, column > DOCS)
        extra = jnp.where(free, 0.0, NEGATIVE).astype(LOW)
        return jnp.concatenate([jnp.transpose(query), extra], axis=0)


HALF = BLOCK // 2


def pieces_of(slots):
    whole = [(s, 0, BLOCK, 0) for s in slots[:-1]]
    return whole + [(slots[-1], 0, HALF, 0), (slots[-1], HALF, HALF, HALF)]


def piece_rows(piece):
    return pl.ds(pl.multiple_of(piece[0] * BLOCK + piece[1], HALF), piece[2])


def plus(total, part, begin):
    if begin == 0:
        return total + part
    return jnp.concatenate([total[:, :begin], total[:, begin:] + part], axis=1)


def score_blocks(keys, pieces, query_wide):
    causal = lax.broadcasted_iota(jnp.int32, (HALF, HALF), 0) <= lax.broadcasted_iota(
        jnp.int32, (HALF, HALF), 1
    )
    result = []
    for piece in pieces:
        scores = dot(keys[piece_rows(piece), :], query_wide[:, piece[3] :])
        if piece[2] == HALF:
            corner = jnp.where(causal, scores[:, :HALF], NEGATIVE)
            scores = jnp.concatenate([corner, scores[:, HALF:]], axis=1) if piece[3] == 0 else corner
        result.append(scores)
    return result


def softmax_blocks(pieces, scores):
    top = jnp.max(scores[0], axis=0, keepdims=True)
    for piece, s in zip(pieces[1:], scores[1:]):
        begin = piece[3]
        most = jnp.maximum(top[:, begin:], jnp.max(s, axis=0, keepdims=True))
        top = most if begin == 0 else jnp.concatenate([top[:, :begin], most], axis=1)
    top = top * SCALE_LOG2
    probs = [jnp.exp2(s * SCALE_LOG2 - top[:, piece[3] :]) for piece, s in zip(pieces, scores)]
    total = jnp.zeros_like(top)
    for piece, p in zip(pieces, probs):
        total = plus(total, jnp.sum(p, axis=0, keepdims=True), piece[3])
    return top, total, probs


def weigh(columns, piece, weights):
    return dot(columns[piece[0], :, piece[1] : piece[1] + piece[2]], weights)


def finish_block(pieces, probs, query, grad, values, keys_t, values_t, add):
    out_t = jnp.zeros((HEAD_DIM, BLOCK), jnp.float32)
    for piece, p in zip(pieces, probs):
        out_t = plus(out_t, weigh(values_t, piece, p), piece[3])
    grad_t = jnp.transpose(grad)
    delta = jnp.sum(grad_t.astype(jnp.float32) * out_t, axis=0, keepdims=True)
    query_t = jnp.zeros((HEAD_DIM, BLOCK), jnp.float32)
    for i, (piece, p) in enumerate(zip(pieces, probs)):
        begin = piece[3]
        prob_grad = dot(values(piece), grad_t[:, begin:])
        score_grad = (p.astype(jnp.float32) * (prob_grad - delta[:, begin:])).astype(LOW)
        query_t = plus(query_t, weigh(keys_t, piece, score_grad), begin)
        add(i, piece, dot(score_grad, query[begin:]), dot(p, grad[begin:]))
    return jnp.transpose(out_t), jnp.transpose(query_t * SCALE)


def halos(x, key_halo, value_halo, qd_halo):
    key_halo[...] = x[PER_BLOCK:, :CHUNK]
    value_halo[...] = x[PER_BLOCK:, CHUNK : 2 * CHUNK]
    qd_halo[...] = x[:FIRST, 2 * CHUNK : 4 * CHUNK]


def last_block(docs, x, od, part, picks, keys, keys_t, values_t):
    for b in range(GROUP):
        sent = x[b * PER_BLOCK : (b + 1) * PER_BLOCK, 4 * CHUNK :].astype(jnp.float32)
        lines = jnp.max(sent, axis=0)
        for i in range(2):
            picks[2 * b + i] = jnp.max(lines[i : i + 1]).astype(jnp.int32)
    marks = Marks(docs)
    for b in range(GROUP):
        key = part_of(x, b, 0)
        keys[pl.ds(b * BLOCK, BLOCK), :HEAD_DIM] = key
        keys[pl.ds(b * BLOCK, BLOCK), HEAD_DIM:] = marks.keys(REACH + b)
        keys_t[b] = jnp.transpose(key)
        values_t[b] = jnp.transpose(part_of(x, b, 1))
    own = GROUP - 1
    query, grad = part_of(x, own, 2), part_of(x, own, 3)
    query_wide = marks.wide_t(query, REACH + own)
    slots = [own - picks[2 * own], own - picks[2 * own + 1], own]
    pieces = pieces_of(slots)
    _, total, probs = softmax_blocks(pieces, score_blocks(keys, pieces, query_wide))
    inverse = 1.0 / total
    probs = [(p * inverse[:, piece[3] :]).astype(LOW) for piece, p in zip(pieces, probs)]
    unused = own * (own - 1) // 2 - slots[0] - slots[1]
    zero = jnp.zeros((BLOCK, HEAD_DIM), LOW)
    put_part(part, unused, 0, zero)
    put_part(part, unused, 1, zero)

    def values(piece):
        first, count = piece[1] // CHUNK, piece[2] // CHUNK
        at = pl.ds(pl.multiple_of(piece[0] * PER_BLOCK, PER_BLOCK) + first, count)
        return x[at, CHUNK : 2 * CHUNK].reshape(piece[2], HEAD_DIM)

    def add(i, piece, key_part, value_part):
        put_part(part, piece[0], 0, key_part * SCALE, piece[1])
        put_part(part, piece[0], 1, value_part, piece[1])

    out, query_grad = finish_block(
        pieces, probs, query, grad, values, keys_t, values_t, add
    )
    put_part(od, 0, 0, out)
    put_part(od, 0, 1, query_grad)


def window_slots(picks, j):
    own = REACH + j
    return [own - picks[2 * j], own - picks[2 * j + 1], own]


def piece_at(j, i, piece):
    return 3 * j + min(i, 2), pl.ds(piece[1], piece[2]), pl.ds(piece[3], BLOCK - piece[3])


def totals(picks, docs, x, key_halo, stats, probs_out, keys, values_t):
    marks = Marks(docs)
    for b in range(2 * REACH):
        key = part_of(x, b - REACH, 0) if b >= REACH else key_halo[
            pl.ds(b * PER_BLOCK, PER_BLOCK)
        ].reshape(BLOCK, HEAD_DIM)
        keys[pl.ds(b * BLOCK, BLOCK), :HEAD_DIM] = key
        keys[pl.ds(b * BLOCK, BLOCK), HEAD_DIM:] = marks.keys(b)
    for b in range(REACH):
        values_t[b] = jnp.transpose(part_of(x, b, 1))
    stats[...] = jnp.zeros_like(stats)
    column = lax.broadcasted_iota(jnp.int32, (1, BLOCK), 1)
    line = jnp.zeros((1, BLOCK), jnp.int32)
    for i in range(2 * REACH):
        line = jnp.where(column == i, picks[i], line)
    stats[6:7, :] = line.astype(jnp.float32)
    def scores_of(j):
        query_wide = marks.wide_t(part_of(x, j, 2), REACH + j)
        slots = window_slots(picks, j)
        pieces = pieces_of(slots)
        return pieces, score_blocks(keys, pieces, query_wide)

    ahead = scores_of(0)
    for j in range(REACH):
        pieces, scores = ahead
        if j + 1 < REACH:
            ahead = scores_of(j + 1)
        top, total, probs = softmax_blocks(pieces, scores)
        probs = [p.astype(LOW) for p in probs]
        stats[j : j + 1, :] = top + jnp.log2(total)
        stats[8 + j : 9 + j, :] = 1.0 / total
        local_t = jnp.zeros((HEAD_DIM, BLOCK), jnp.float32)
        for i, (piece, p) in enumerate(zip(pieces, probs)):
            probs_out[piece_at(j, i, piece)] = p
            if i >= 2:
                local_t = plus(local_t, weigh(values_t, (j, *piece[1:]), p), piece[3])
            elif j > 0:
                here = jnp.where(piece[0] >= REACH, 1.0, 0.0)
                slot = jnp.maximum(piece[0] - REACH, 0)
                local_t += here * weigh(values_t, (slot, *piece[1:]), p)
        grad_t = jnp.transpose(part_of(x, j, 3))
        delta = jnp.sum(grad_t.astype(jnp.float32) * local_t, axis=0, keepdims=True)
        stats[REACH + j : REACH + j + 1, :] = delta / total


def first_blocks(
    picks, x, key_halo, value_halo, stats, probs_in, od, part,
    values, keys_t, values_t, key_sum, value_sum,
):
    for b in range(2 * REACH):
        rows = pl.ds(b * BLOCK, BLOCK)
        if b < REACH:
            at = pl.ds(b * PER_BLOCK, PER_BLOCK)
            key = key_halo[at].reshape(BLOCK, HEAD_DIM)
            value = value_halo[at].reshape(BLOCK, HEAD_DIM)
        else:
            key, value = part_of(x, b - REACH, 0), part_of(x, b - REACH, 1)
        values[rows, :] = value
        keys_t[b] = jnp.transpose(key)
        values_t[b] = jnp.transpose(value)
    key_sum[...] = jnp.zeros_like(key_sum)
    value_sum[...] = jnp.zeros_like(value_sum)
    for j in range(REACH):
        query, grad = part_of(x, j, 2), part_of(x, j, 3)
        pieces = pieces_of(window_slots(picks, j))
        inverse = stats[8 + j : 9 + j, :]
        probs = [
            (probs_in[piece_at(j, i, piece)].astype(jnp.float32) * inverse[:, piece[3] :]).astype(LOW)
            for i, piece in enumerate(pieces)
        ]

        def add(i, piece, key_part, value_part):
            if j == 0 and i < 2:
                return
            key_sum[piece_rows(piece), :] += key_part
            value_sum[piece_rows(piece), :] += value_part

        out, query_grad = finish_block(
            pieces, probs, query, grad, lambda piece: values[piece_rows(piece), :],
            keys_t, values_t, add,
        )
        put_part(od, j, 0, out)
        put_part(od, j, 1, query_grad)
    for b in range(REACH):
        rows = pl.ds((REACH + b) * BLOCK, BLOCK)
        put_part(part, b, 0, key_sum[rows, :] * SCALE)
        put_part(part, b, 1, value_sum[rows, :])


def later_queries(
    picks, docs, x, qd_next, stats, last_od, last_part, keys, first_od, first_part, y,
    key_sum, value_sum,
):
    y[:FIRST, : 2 * CHUNK] = first_od[...]
    y[FIRST:, : 2 * CHUNK] = last_od[...]
    marks = Marks(docs)
    key_sum[...] = jnp.zeros_like(key_sum)
    value_sum[...] = jnp.zeros_like(value_sum)
    for j in range(REACH):
        query, grad = part_of(qd_next, j, 0), part_of(qd_next, j, 1)
        query_wide = marks.wide_t(query, REACH + GROUP + j)
        log_total = stats[j : j + 1, :]
        delta = stats[REACH + j : REACH + j + 1, :]
        first, second = [jnp.maximum(picks[6, 2 * j + i].astype(jnp.int32), 1) for i in range(2)]
        if j == 0:
            chosen = [(GROUP - first, log_total), (GROUP - second, log_total)]
        else:
            chosen = []
            for offset in range(j + 1, REACH + 1):
                used = jnp.logical_or(first == offset, second == offset)
                chosen.append((GROUP + j - offset, jnp.where(used, log_total, -NEGATIVE)))
        grad_t = jnp.transpose(grad)
        probs, products = [], []
        for b, shift in chosen:
            scores = dot(keys[rows_of(b), :], query_wide)
            p = jnp.exp2(scores * SCALE_LOG2 - shift)
            product = p * dot(part_of(x, b, 1), grad_t)
            delta = delta + jnp.sum(product, axis=0, keepdims=True)
            probs.append(p)
            products.append(product)
        for (b, _), p, product in zip(chosen, probs, products):
            score_grad = (product - p * delta).astype(LOW)
            key_sum[rows_of(b - 1), :] += dot(score_grad, query)
            value_sum[rows_of(b - 1), :] += dot(p.astype(LOW), grad)
    for b in range(GROUP):
        for array, ref, scale in ((0, key_sum, SCALE), (1, value_sum, 1.0)):
            total = part_of(last_part, b, array).astype(jnp.float32)
            if b < REACH:
                total = total + part_of(first_part, b, array).astype(jnp.float32)
            if b > 0:
                total = total + ref[pl.ds((b - 1) * BLOCK, BLOCK), :] * scale
            put_part(y, b, 2 + array, total)


def params(mib):
    return pltpu.CompilerParams(vmem_limit_bytes=mib * MIB)


def cost(pairs, products, mib):
    area = pairs * BLOCK * BLOCK
    return pl.CostEstimate(
        flops=2 * products * area * HEAD_DIM, bytes_accessed=mib * MIB, transcendentals=area
    )


def chunks(count, arrays):
    return (count, arrays * CHUNK, HEAD_DIM)


def array(shape, dtype=LOW):
    return jax.ShapeDtypeStruct(shape, dtype)


FIRST = REACH * PER_BLOCK


def run_halos(x):
    one, two = array((FIRST, CHUNK, HEAD_DIM)), array(chunks(FIRST, 2))
    return pl.pallas_call(
        halos,
        out_shape=(one, one, two),
        in_specs=[VMEM],
        out_specs=(VMEM,) * 3,
        compiler_params=params(8),
        cost_estimate=cost(0, 0, 3),
        name="halos",
    )(x)


def run_last(docs, x):
    wide, high = 2 * HEAD_DIM, GROUP * BLOCK
    return pl.pallas_call(
        last_block,
        out_shape=(
            array(chunks(PER_BLOCK, 2)),
            array(chunks(HEADS, 2)),
            array((2 * GROUP,), jnp.int32),
            array((high, wide)),
        ),
        in_specs=[VMEM, VMEM],
        out_specs=(VMEM, VMEM, SMEM, VMEM),
        scratch_shapes=[
            pltpu.VMEM((GROUP, HEAD_DIM, BLOCK), LOW),
            pltpu.VMEM((GROUP, HEAD_DIM, BLOCK), LOW),
        ],
        compiler_params=params(24),
        cost_estimate=cost(3, 6, 3),
        name="last_block",
    )(docs, x)


def run_totals(picks, docs, x, key_halo):
    wide, high = 2 * HEAD_DIM, 2 * REACH * BLOCK
    return pl.pallas_call(
        totals,
        out_shape=(array((16, BLOCK), jnp.float32), array((3 * REACH, BLOCK, BLOCK))),
        in_specs=[SMEM, VMEM, VMEM, VMEM],
        out_specs=(VMEM, VMEM),
        scratch_shapes=[
            pltpu.VMEM((high, wide), LOW),
            pltpu.VMEM((REACH, HEAD_DIM, BLOCK), LOW),
        ],
        compiler_params=params(24),
        cost_estimate=cost(9, 2, 2),
        name="totals",
    )(picks, docs, x, key_halo)


def run_first(picks, x, key_halo, value_halo, stats, probs):
    high = 2 * REACH * BLOCK
    return pl.pallas_call(
        first_blocks,
        out_shape=(array(chunks(FIRST, 2)),) * 2,
        in_specs=[SMEM] + [VMEM] * 5,
        out_specs=(VMEM, VMEM),
        scratch_shapes=[
            pltpu.VMEM((high, HEAD_DIM), LOW),
            pltpu.VMEM((2 * REACH, HEAD_DIM, BLOCK), LOW),
            pltpu.VMEM((2 * REACH, HEAD_DIM, BLOCK), LOW),
            pltpu.VMEM((high, HEAD_DIM), jnp.float32),
            pltpu.VMEM((high, HEAD_DIM), jnp.float32),
        ],
        compiler_params=params(32),
        cost_estimate=cost(9, 6, 5),
        name="first_blocks",
    )(picks, x, key_halo, value_halo, stats, probs)


def run_later(docs, x, qd_next, stats, *parts):
    high = REACH * BLOCK
    return pl.pallas_call(
        later_queries,
        out_shape=array(chunks(HEADS, 4)),
        in_specs=[SMEM] + [VMEM] * 9,
        out_specs=VMEM,
        scratch_shapes=[
            pltpu.VMEM((high, HEAD_DIM), jnp.float32),
            pltpu.VMEM((high, HEAD_DIM), jnp.float32),
        ],
        compiler_params=params(24),
        cost_estimate=cost(5, 4, 5),
        name="later_queries",
    )(stats, docs, x, qd_next, stats, *parts)


SENT = 4 * CHUNK + 16


def pack(picks_sent, k_rows, v_rows, q_rows, d_rows, packed, rows, done, picks, picks_done):
    sources = (k_rows, v_rows, q_rows, d_rows)
    copies = [pltpu.make_async_copy(r, rows.at[i], done.at[i]) for i, r in enumerate(sources)]
    picks_copy = pltpu.make_async_copy(picks_sent, picks, picks_done)
    for copy in copies + [picks_copy]:
        copy.start()
    picks_copy.wait()
    line = lax.broadcasted_iota(jnp.int32, (16, HEAD_DIM), 0)
    mine = lax.axis_index("h")
    for k in range(GROUP):
        pair = jnp.where(line == 0, picks[0, 0, k], picks[0, 1, k]).astype(jnp.float32)
        for h in range(PER_BLOCK):
            packed[k, h, 4 * CHUNK :] = jnp.where(mine == h, pair, 0.0).astype(LOW)
    for i, copy in enumerate(copies):
        copy.wait()
        for k in range(GROUP):
            for h in range(PER_BLOCK):
                start = (h * GROUP + k) * HEAD_DIM
                packed[k, h, i * CHUNK : (i + 1) * CHUNK] = rows[i, :, start : start + HEAD_DIM]


def unpack(packed, out, q_rows, k_rows, v_rows, rows, done):
    copies = []
    for i, target in enumerate((out, q_rows, k_rows, v_rows)):
        for k in range(GROUP):
            for h in range(PER_BLOCK):
                start = (h * GROUP + k) * HEAD_DIM
                rows[i, :, start : start + HEAD_DIM] = packed[k, h, i * CHUNK : (i + 1) * CHUNK]
        copies.append(pltpu.make_async_copy(rows.at[i], target, done.at[i]))
        copies[-1].start()
    for copy in copies:
        copy.wait()


HBM = pl.BlockSpec(memory_space=pltpu.HBM)
STAGING = [pltpu.VMEM((4, CHUNK, HEADS * HEAD_DIM), LOW), pltpu.SemaphoreType.DMA((4,))]


def run_pack(picks, *rows):
    packed = pl.pallas_call(
        pack,
        out_shape=array((GROUP, PER_BLOCK, SENT, HEAD_DIM)),
        in_specs=[HBM] * 5,
        out_specs=VMEM,
        scratch_shapes=STAGING
        + [pltpu.SMEM((1, 2, GROUP), jnp.int32), pltpu.SemaphoreType.DMA],
        compiler_params=params(16),
        cost_estimate=cost(0, 0, 4),
        name="pack",
    )(*[pltpu.with_memory_space_constraint(r, pltpu.HBM) for r in (picks, *rows)])
    return packed.reshape(HEADS, SENT, HEAD_DIM)


def run_unpack(packed):
    return pl.pallas_call(
        unpack,
        out_shape=(array((CHUNK, HEADS * HEAD_DIM)),) * 4,
        in_specs=[VMEM],
        out_specs=(HBM,) * 4,
        scratch_shapes=STAGING,
        compiler_params=params(16),
        cost_estimate=cost(0, 0, 4),
        name="unpack",
    )(packed.reshape(GROUP, PER_BLOCK, 4 * CHUNK, HEAD_DIM))


def per_device(queries, key_rows, value_rows, out_grad, doc_ids, picks):
    plane = lax.axis_index("z")
    planes = lax.axis_size("z")
    forward = [(i, i + 1) for i in range(planes - 1)]
    backward = [(i + 1, i) for i in range(planes - 1)]

    def exchange(packed):
        return lax.all_to_all(packed, ("y", "h"), split_axis=0, concat_axis=0)

    x = exchange(run_pack(jnp.swapaxes(picks, 1, 2), key_rows, value_rows, queries, out_grad))

    edge = jnp.full((REACH * BLOCK,), DOCS, jnp.int32)
    docs = jnp.concatenate([edge, doc_ids, edge])
    docs = lax.dynamic_slice_in_dim(
        docs, plane * (GROUP * BLOCK), (2 * REACH + GROUP) * BLOCK, 0
    )
    docs = docs.astype(jnp.float32).reshape(-1, HEAD_DIM)

    key_halo, value_halo, qd_next = run_halos(x)
    key_halo = lax.ppermute(key_halo, "z", forward)
    value_halo = lax.ppermute(value_halo, "z", forward)
    qd_next = lax.ppermute(qd_next, "z", backward)

    last_od, last_part, picks_here, keys = run_last(docs, x)
    stats, probs = run_totals(picks_here, docs, x, key_halo)
    stats_next = lax.ppermute(stats[:8], "z", backward)
    first = run_first(picks_here, x, key_halo, value_halo, stats, probs)
    y = run_later(docs, x, qd_next, stats_next, last_od, last_part, keys, *first)
    return tuple(run_unpack(exchange(y)))


def solution(mesh):
    planes = mesh.shape["seq"] // GROUP
    parts = Mesh(mesh.devices.reshape(planes, GROUP, mesh.shape["head"]), ("z", "y", "h"))
    rows = P(("z", "y", "h"), None)
    return jax.shard_map(
        per_device,
        mesh=parts,
        in_specs=(rows, rows, rows, rows, P(), P(("z", "y"), "h", None)),
        out_specs=(rows,) * 4,
        check_vma=False,
    )
```

```python
import math

import jax
import jax.numpy as jnp
from jax import lax
from jax.experimental import pallas as pl
from jax.experimental.pallas import tpu as pltpu
from jax.sharding import Mesh
from jax.sharding import PartitionSpec as P

HEADS = 32
HEAD_DIM = 128
BLOCK = 512
REACH = 3
GROUP = 4
DOCS = 16
CHUNK = 64
PER_BLOCK = BLOCK // CHUNK
NEGATIVE = -1e30
SCALE = HEAD_DIM ** (-0.5)
SCALE_LOG2 = SCALE * math.log2(math.e)
LOW = jnp.bfloat16
MIB = 1024 * 1024

NT = (((1,), (1,)), ((), ()))
NN = (((1,), (0,)), ((), ()))
VMEM = pl.BlockSpec(memory_space=pltpu.VMEM)
SMEM = pl.BlockSpec(memory_space=pltpu.SMEM)


def dot(a, b, dims=NN):
    return lax.dot_general(a, b, dims, preferred_element_type=jnp.float32)


def part_of(ref, block, array):
    start = pl.multiple_of(block * PER_BLOCK, PER_BLOCK)
    rows = ref[pl.ds(start, PER_BLOCK), array * CHUNK : (array + 1) * CHUNK]
    return rows.reshape(BLOCK, HEAD_DIM)


def put_part(ref, block, array, rows, first=0):
    start = pl.multiple_of(block * PER_BLOCK, PER_BLOCK) + first // CHUNK
    count = rows.shape[0] // CHUNK
    rows = rows.astype(LOW).reshape(count, CHUNK, HEAD_DIM)
    ref[pl.ds(start, count), array * CHUNK : (array + 1) * CHUNK] = rows


def rows_of(block):
    return pl.ds(pl.multiple_of(block * BLOCK, BLOCK), BLOCK)


class Marks:
    def __init__(self, docs):
        self.rows = docs
        self.docs = jnp.transpose(docs[...])
        self.lane = lax.broadcasted_iota(jnp.int32, (128, 128), 1).astype(jnp.float32)

    def same(self, block):
        columns = [self.docs[:, 4 * block + i : 4 * block + i + 1] for i in range(4)]
        return [jnp.broadcast_to(c, (128, 128)) == self.lane for c in columns]

    def keys(self, block):
        return jnp.concatenate([jnp.where(s, 1.0, 0.0).astype(LOW) for s in self.same(block)], axis=0)

    def wide_t(self, query, block):
        rows = [self.rows[4 * block + i : 4 * block + i + 1, :] for i in range(4)]
        docs = jnp.broadcast_to(jnp.concatenate(rows, axis=1), (HEAD_DIM, BLOCK))
        column = lax.broadcasted_iota(jnp.int32, (HEAD_DIM, BLOCK), 0).astype(jnp.float32)
        free = jnp.logical_or(docs == column, column > DOCS)
        extra = jnp.where(free, 0.0, NEGATIVE).astype(LOW)
        return jnp.concatenate([jnp.transpose(query), extra], axis=0)


HALF = BLOCK // 2


def pieces_of(slots):
    whole = [(s, 0, BLOCK, 0) for s in slots[:-1]]
    return whole + [(slots[-1], 0, HALF, 0), (slots[-1], HALF, HALF, HALF)]


def piece_rows(piece):
    return pl.ds(pl.multiple_of(piece[0] * BLOCK + piece[1], HALF), piece[2])


def plus(total, part, begin):
    if begin == 0:
        return total + part
    return jnp.concatenate([total[:, :begin], total[:, begin:] + part], axis=1)


def score_blocks(keys, pieces, query_wide):
    causal = lax.broadcasted_iota(jnp.int32, (HALF, HALF), 0) <= lax.broadcasted_iota(
        jnp.int32, (HALF, HALF), 1
    )
    result = []
    for piece in pieces:
        scores = dot(keys[piece_rows(piece), :], query_wide[:, piece[3] :])
        if piece[2] == HALF:
            corner = jnp.where(causal, scores[:, :HALF], NEGATIVE)
            scores = jnp.concatenate([corner, scores[:, HALF:]], axis=1) if piece[3] == 0 else corner
        result.append(scores)
    return result


def softmax_blocks(pieces, scores):
    top = jnp.max(scores[0], axis=0, keepdims=True)
    for piece, s in zip(pieces[1:], scores[1:]):
        begin = piece[3]
        most = jnp.maximum(top[:, begin:], jnp.max(s, axis=0, keepdims=True))
        top = most if begin == 0 else jnp.concatenate([top[:, :begin], most], axis=1)
    top = top * SCALE_LOG2
    probs = [jnp.exp2(s * SCALE_LOG2 - top[:, piece[3] :]) for piece, s in zip(pieces, scores)]
    total = jnp.zeros_like(top)
    for piece, p in zip(pieces, probs):
        total = plus(total, jnp.sum(p, axis=0, keepdims=True), piece[3])
    return top, total, probs


def weigh(columns, piece, weights):
    return dot(columns[piece[0], :, piece[1] : piece[1] + piece[2]], weights)


def finish_block(pieces, probs, query, grad, values, keys_t, values_t, add):
    out_t = jnp.zeros((HEAD_DIM, BLOCK), jnp.float32)
    for piece, p in zip(pieces, probs):
        out_t = plus(out_t, weigh(values_t, piece, p), piece[3])
    grad_t = jnp.transpose(grad)
    delta = jnp.sum(grad_t.astype(jnp.float32) * out_t, axis=0, keepdims=True)
    query_t = jnp.zeros((HEAD_DIM, BLOCK), jnp.float32)
    for i, (piece, p) in enumerate(zip(pieces, probs)):
        begin = piece[3]
        prob_grad = dot(values(piece), grad_t[:, begin:])
        score_grad = (p.astype(jnp.float32) * (prob_grad - delta[:, begin:])).astype(LOW)
        query_t = plus(query_t, weigh(keys_t, piece, score_grad), begin)
        add(i, piece, dot(score_grad, query[begin:]), dot(p, grad[begin:]))
    return jnp.transpose(out_t), jnp.transpose(query_t * SCALE)


def halos(x, key_halo, value_halo, qd_halo):
    key_halo[...] = x[PER_BLOCK:, :CHUNK]
    value_halo[...] = x[PER_BLOCK:, CHUNK : 2 * CHUNK]
    qd_halo[...] = x[:FIRST, 2 * CHUNK : 4 * CHUNK]


def last_block(docs, x, od, part, picks, keys, keys_t, values_t):
    for b in range(GROUP):
        sent = x[b * PER_BLOCK : (b + 1) * PER_BLOCK, 4 * CHUNK :].astype(jnp.float32)
        lines = jnp.max(sent, axis=0)
        for i in range(2):
            picks[2 * b + i] = jnp.max(lines[i : i + 1]).astype(jnp.int32)
    marks = Marks(docs)
    for b in range(GROUP):
        key = part_of(x, b, 0)
        keys[pl.ds(b * BLOCK, BLOCK), :HEAD_DIM] = key
        keys[pl.ds(b * BLOCK, BLOCK), HEAD_DIM:] = marks.keys(REACH + b)
        keys_t[b] = jnp.transpose(key)
        values_t[b] = jnp.transpose(part_of(x, b, 1))
    own = GROUP - 1
    query, grad = part_of(x, own, 2), part_of(x, own, 3)
    query_wide = marks.wide_t(query, REACH + own)
    slots = [own - picks[2 * own], own - picks[2 * own + 1], own]
    pieces = pieces_of(slots)
    _, total, probs = softmax_blocks(pieces, score_blocks(keys, pieces, query_wide))
    inverse = 1.0 / total
    probs = [(p * inverse[:, piece[3] :]).astype(LOW) for piece, p in zip(pieces, probs)]
    unused = own * (own - 1) // 2 - slots[0] - slots[1]
    zero = jnp.zeros((BLOCK, HEAD_DIM), LOW)
    put_part(part, unused, 0, zero)
    put_part(part, unused, 1, zero)

    def values(piece):
        first, count = piece[1] // CHUNK, piece[2] // CHUNK
        at = pl.ds(pl.multiple_of(piece[0] * PER_BLOCK, PER_BLOCK) + first, count)
        return x[at, CHUNK : 2 * CHUNK].reshape(piece[2], HEAD_DIM)

    def add(i, piece, key_part, value_part):
        put_part(part, piece[0], 0, key_part * SCALE, piece[1])
        put_part(part, piece[0], 1, value_part, piece[1])

    out, query_grad = finish_block(
        pieces, probs, query, grad, values, keys_t, values_t, add
    )
    put_part(od, 0, 0, out)
    put_part(od, 0, 1, query_grad)


def window_slots(picks, j):
    own = REACH + j
    return [own - picks[2 * j], own - picks[2 * j + 1], own]


def piece_at(j, i, piece):
    return 3 * j + min(i, 2), pl.ds(piece[1], piece[2]), pl.ds(piece[3], BLOCK - piece[3])


def totals(picks, docs, x, key_halo, stats, probs_out, keys, values_t):
    marks = Marks(docs)
    for b in range(2 * REACH):
        key = part_of(x, b - REACH, 0) if b >= REACH else key_halo[
            pl.ds(b * PER_BLOCK, PER_BLOCK)
        ].reshape(BLOCK, HEAD_DIM)
        keys[pl.ds(b * BLOCK, BLOCK), :HEAD_DIM] = key
        keys[pl.ds(b * BLOCK, BLOCK), HEAD_DIM:] = marks.keys(b)
    for b in range(REACH):
        values_t[b] = jnp.transpose(part_of(x, b, 1))
    stats[...] = jnp.zeros_like(stats)
    column = lax.broadcasted_iota(jnp.int32, (1, BLOCK), 1)
    line = jnp.zeros((1, BLOCK), jnp.int32)
    for i in range(2 * REACH):
        line = jnp.where(column == i, picks[i], line)
    stats[6:7, :] = line.astype(jnp.float32)
    def scores_of(j):
        query_wide = marks.wide_t(part_of(x, j, 2), REACH + j)
        slots = window_slots(picks, j)
        pieces = pieces_of(slots)
        return pieces, score_blocks(keys, pieces, query_wide)

    ahead = scores_of(0)
    for j in range(REACH):
        pieces, scores = ahead
        if j + 1 < REACH:
            ahead = scores_of(j + 1)
        top, total, probs = softmax_blocks(pieces, scores)
        probs = [p.astype(LOW) for p in probs]
        stats[j : j + 1, :] = top + jnp.log2(total)
        stats[8 + j : 9 + j, :] = 1.0 / total
        local_t = jnp.zeros((HEAD_DIM, BLOCK), jnp.float32)
        for i, (piece, p) in enumerate(zip(pieces, probs)):
            probs_out[piece_at(j, i, piece)] = p
            if i >= 2:
                local_t = plus(local_t, weigh(values_t, (j, *piece[1:]), p), piece[3])
            elif j > 0:
                here = jnp.where(piece[0] >= REACH, 1.0, 0.0)
                slot = jnp.maximum(piece[0] - REACH, 0)
                local_t += here * weigh(values_t, (slot, *piece[1:]), p)
        grad_t = jnp.transpose(part_of(x, j, 3))
        delta = jnp.sum(grad_t.astype(jnp.float32) * local_t, axis=0, keepdims=True)
        stats[REACH + j : REACH + j + 1, :] = delta / total


def first_blocks(
    picks, x, key_halo, value_halo, stats, probs_in, od, part,
    values, keys_t, values_t, key_sum, value_sum,
):
    for b in range(2 * REACH):
        rows = pl.ds(b * BLOCK, BLOCK)
        if b < REACH:
            at = pl.ds(b * PER_BLOCK, PER_BLOCK)
            key = key_halo[at].reshape(BLOCK, HEAD_DIM)
            value = value_halo[at].reshape(BLOCK, HEAD_DIM)
        else:
            key, value = part_of(x, b - REACH, 0), part_of(x, b - REACH, 1)
        values[rows, :] = value
        keys_t[b] = jnp.transpose(key)
        values_t[b] = jnp.transpose(value)
    key_sum[...] = jnp.zeros_like(key_sum)
    value_sum[...] = jnp.zeros_like(value_sum)
    for j in range(REACH):
        query, grad = part_of(x, j, 2), part_of(x, j, 3)
        pieces = pieces_of(window_slots(picks, j))
        inverse = stats[8 + j : 9 + j, :]
        probs = [
            (probs_in[piece_at(j, i, piece)].astype(jnp.float32) * inverse[:, piece[3] :]).astype(LOW)
            for i, piece in enumerate(pieces)
        ]

        def add(i, piece, key_part, value_part):
            if j == 0 and i < 2:
                return
            key_sum[piece_rows(piece), :] += key_part
            value_sum[piece_rows(piece), :] += value_part

        out, query_grad = finish_block(
            pieces, probs, query, grad, lambda piece: values[piece_rows(piece), :],
            keys_t, values_t, add,
        )
        put_part(od, j, 0, out)
        put_part(od, j, 1, query_grad)
    for b in range(REACH):
        rows = pl.ds((REACH + b) * BLOCK, BLOCK)
        put_part(part, b, 0, key_sum[rows, :] * SCALE)
        put_part(part, b, 1, value_sum[rows, :])


def later_queries(
    picks, docs, x, qd_next, stats, last_od, last_part, keys, first_od, first_part, y,
    key_sum, value_sum,
):
    y[:FIRST, : 2 * CHUNK] = first_od[...]
    y[FIRST:, : 2 * CHUNK] = last_od[...]
    marks = Marks(docs)
    key_sum[...] = jnp.zeros_like(key_sum)
    value_sum[...] = jnp.zeros_like(value_sum)
    for j in range(REACH):
        query, grad = part_of(qd_next, j, 0), part_of(qd_next, j, 1)
        query_wide = marks.wide_t(query, REACH + GROUP + j)
        log_total = stats[j : j + 1, :]
        delta = stats[REACH + j : REACH + j + 1, :]
        first, second = [jnp.maximum(picks[6, 2 * j + i].astype(jnp.int32), 1) for i in range(2)]
        if j == 0:
            chosen = [(GROUP - first, log_total), (GROUP - second, log_total)]
        else:
            chosen = []
            for offset in range(j + 1, REACH + 1):
                used = jnp.logical_or(first == offset, second == offset)
                chosen.append((GROUP + j - offset, jnp.where(used, log_total, -NEGATIVE)))
        grad_t = jnp.transpose(grad)
        probs, products = [], []
        for b, shift in chosen:
            scores = dot(keys[rows_of(b), :], query_wide)
            p = jnp.exp2(scores * SCALE_LOG2 - shift)
            product = p * dot(part_of(x, b, 1), grad_t)
            delta = delta + jnp.sum(product, axis=0, keepdims=True)
            probs.append(p)
            products.append(product)
        for (b, _), p, product in zip(chosen, probs, products):
            score_grad = (product - p * delta).astype(LOW)
            key_sum[rows_of(b - 1), :] += dot(score_grad, query)
            value_sum[rows_of(b - 1), :] += dot(p.astype(LOW), grad)
    for b in range(GROUP):
        for array, ref, scale in ((0, key_sum, SCALE), (1, value_sum, 1.0)):
            total = part_of(last_part, b, array).astype(jnp.float32)
            if b < REACH:
                total = total + part_of(first_part, b, array).astype(jnp.float32)
            if b > 0:
                total = total + ref[pl.ds((b - 1) * BLOCK, BLOCK), :] * scale
            put_part(y, b, 2 + array, total)


def params(mib):
    return pltpu.CompilerParams(vmem_limit_bytes=mib * MIB)


def cost(pairs, products, mib):
    area = pairs * BLOCK * BLOCK
    return pl.CostEstimate(
        flops=2 * products * area * HEAD_DIM, bytes_accessed=mib * MIB, transcendentals=area
    )


def chunks(count, arrays):
    return (count, arrays * CHUNK, HEAD_DIM)


def array(shape, dtype=LOW):
    return jax.ShapeDtypeStruct(shape, dtype)


FIRST = REACH * PER_BLOCK


def run_halos(x):
    one, two = pltpu.VMEM((FIRST, CHUNK, HEAD_DIM), LOW), pltpu.VMEM(chunks(FIRST, 2), LOW)
    return pl.pallas_call(
        halos,
        out_shape=(one, one, two),
        in_specs=[VMEM],
        out_specs=(VMEM,) * 3,
        compiler_params=params(8),
        cost_estimate=cost(0, 0, 3),
        name="halos",
    )(x)


def run_last(docs, x):
    wide, high = 2 * HEAD_DIM, GROUP * BLOCK
    return pl.pallas_call(
        last_block,
        out_shape=(
            array(chunks(PER_BLOCK, 2)),
            array(chunks(HEADS, 2)),
            array((2 * GROUP,), jnp.int32),
            array((high, wide)),
        ),
        in_specs=[VMEM, VMEM],
        out_specs=(VMEM, VMEM, SMEM, VMEM),
        scratch_shapes=[
            pltpu.VMEM((GROUP, HEAD_DIM, BLOCK), LOW),
            pltpu.VMEM((GROUP, HEAD_DIM, BLOCK), LOW),
        ],
        compiler_params=params(16),
        cost_estimate=cost(3, 6, 3),
        name="last_block",
    )(docs, x)


def run_totals(picks, docs, x, key_halo):
    wide, high = 2 * HEAD_DIM, 2 * REACH * BLOCK
    return pl.pallas_call(
        totals,
        out_shape=(array((16, BLOCK), jnp.float32), array((3 * REACH, BLOCK, BLOCK))),
        in_specs=[SMEM, VMEM, VMEM, VMEM],
        out_specs=(VMEM, VMEM),
        scratch_shapes=[
            pltpu.VMEM((high, wide), LOW),
            pltpu.VMEM((REACH, HEAD_DIM, BLOCK), LOW),
        ],
        compiler_params=params(20),
        cost_estimate=cost(9, 2, 2),
        name="totals",
    )(picks, docs, x, key_halo)


def run_first(picks, x, key_halo, value_halo, stats, probs):
    high = 2 * REACH * BLOCK
    return pl.pallas_call(
        first_blocks,
        out_shape=(array(chunks(FIRST, 2)),) * 2,
        in_specs=[SMEM] + [VMEM] * 5,
        out_specs=(VMEM, VMEM),
        scratch_shapes=[
            pltpu.VMEM((high, HEAD_DIM), LOW),
            pltpu.VMEM((2 * REACH, HEAD_DIM, BLOCK), LOW),
            pltpu.VMEM((2 * REACH, HEAD_DIM, BLOCK), LOW),
            pltpu.VMEM((high, HEAD_DIM), jnp.float32),
            pltpu.VMEM((high, HEAD_DIM), jnp.float32),
        ],
        compiler_params=params(24),
        cost_estimate=cost(9, 6, 5),
        name="first_blocks",
    )(picks, x, key_halo, pltpu.with_memory_space_constraint(value_halo, pltpu.VMEM), stats, probs)


def run_later(docs, x, qd_next, stats, *parts):
    high = REACH * BLOCK
    return pl.pallas_call(
        later_queries,
        out_shape=array(chunks(HEADS, 4)),
        in_specs=[SMEM] + [VMEM] * 9,
        out_specs=VMEM,
        scratch_shapes=[
            pltpu.VMEM((high, HEAD_DIM), jnp.float32),
            pltpu.VMEM((high, HEAD_DIM), jnp.float32),
        ],
        compiler_params=params(16),
        cost_estimate=cost(5, 4, 5),
        name="later_queries",
    )(stats, docs, x, qd_next, stats, *parts)


SENT = 4 * CHUNK + 16


def pack(picks_sent, k_rows, v_rows, q_rows, d_rows, packed, rows, done, picks, picks_done):
    sources = (k_rows, v_rows, q_rows, d_rows)
    copies = [pltpu.make_async_copy(r, rows.at[i], done.at[i]) for i, r in enumerate(sources)]
    picks_copy = pltpu.make_async_copy(picks_sent, picks, picks_done)
    for copy in copies + [picks_copy]:
        copy.start()
    picks_copy.wait()
    line = lax.broadcasted_iota(jnp.int32, (16, HEAD_DIM), 0)
    mine = lax.axis_index("h")
    for k in range(GROUP):
        pair = jnp.where(line == 0, picks[0, 0, k], picks[0, 1, k]).astype(jnp.float32)
        for h in range(PER_BLOCK):
            packed[k, h, 4 * CHUNK :] = jnp.where(mine == h, pair, 0.0).astype(LOW)
    for i, copy in enumerate(copies):
        copy.wait()
        for k in range(GROUP):
            for h in range(PER_BLOCK):
                start = (h * GROUP + k) * HEAD_DIM
                packed[k, h, i * CHUNK : (i + 1) * CHUNK] = rows[i, :, start : start + HEAD_DIM]


def unpack(packed, out, q_rows, k_rows, v_rows, rows, done):
    copies = []
    for i, target in enumerate((out, q_rows, k_rows, v_rows)):
        for k in range(GROUP):
            for h in range(PER_BLOCK):
                start = (h * GROUP + k) * HEAD_DIM
                rows[i, :, start : start + HEAD_DIM] = packed[k, h, i * CHUNK : (i + 1) * CHUNK]
        copies.append(pltpu.make_async_copy(rows.at[i], target, done.at[i]))
        copies[-1].start()
    for copy in copies:
        copy.wait()


HBM = pl.BlockSpec(memory_space=pltpu.HBM)
STAGING = [pltpu.VMEM((4, CHUNK, HEADS * HEAD_DIM), LOW), pltpu.SemaphoreType.DMA((4,))]


def run_pack(picks, *rows):
    packed = pl.pallas_call(
        pack,
        out_shape=array((GROUP, PER_BLOCK, SENT, HEAD_DIM)),
        in_specs=[HBM] * 5,
        out_specs=VMEM,
        scratch_shapes=STAGING
        + [pltpu.SMEM((1, 2, GROUP), jnp.int32), pltpu.SemaphoreType.DMA],
        compiler_params=params(8),
        cost_estimate=cost(0, 0, 4),
        name="pack",
    )(*[pltpu.with_memory_space_constraint(r, pltpu.HBM) for r in (picks, *rows)])
    return packed.reshape(HEADS, SENT, HEAD_DIM)


def run_unpack(packed):
    return pl.pallas_call(
        unpack,
        out_shape=(array((CHUNK, HEADS * HEAD_DIM)),) * 4,
        in_specs=[VMEM],
        out_specs=(HBM,) * 4,
        scratch_shapes=STAGING,
        compiler_params=params(8),
        cost_estimate=cost(0, 0, 4),
        name="unpack",
    )(packed.reshape(GROUP, PER_BLOCK, 4 * CHUNK, HEAD_DIM))


def per_device(queries, key_rows, value_rows, out_grad, doc_ids, picks):
    plane = lax.axis_index("z")
    planes = lax.axis_size("z")
    forward = [(i, i + 1) for i in range(planes - 1)]
    backward = [(i + 1, i) for i in range(planes - 1)]

    def exchange(packed):
        return lax.all_to_all(packed, ("y", "h"), split_axis=0, concat_axis=0)

    x = exchange(run_pack(jnp.swapaxes(picks, 1, 2), key_rows, value_rows, queries, out_grad))

    edge = jnp.full((REACH * BLOCK,), DOCS, jnp.int32)
    docs = jnp.concatenate([edge, doc_ids, edge])
    docs = lax.dynamic_slice_in_dim(
        docs, plane * (GROUP * BLOCK), (2 * REACH + GROUP) * BLOCK, 0
    )
    docs = docs.astype(jnp.float32).reshape(-1, HEAD_DIM)

    key_halo, value_halo, qd_next = run_halos(x)
    key_halo = lax.ppermute(key_halo, "z", forward)
    value_halo = lax.ppermute(value_halo, "z", forward)
    qd_next = lax.ppermute(qd_next, "z", backward)

    last_od, last_part, picks_here, keys = run_last(docs, x)
    stats, probs = run_totals(picks_here, docs, x, key_halo)
    stats_next = lax.ppermute(stats[:8], "z", backward)
    first = run_first(picks_here, x, key_halo, value_halo, stats, probs)
    y = run_later(docs, x, qd_next, stats_next, last_od, last_part, keys, *first)
    return tuple(run_unpack(exchange(y)))


def solution(mesh):
    planes = mesh.shape["seq"] // GROUP
    parts = Mesh(mesh.devices.reshape(planes, GROUP, mesh.shape["head"]), ("z", "y", "h"))
    rows = P(("z", "y", "h"), None)
    return jax.shard_map(
        per_device,
        mesh=parts,
        in_specs=(rows, rows, rows, rows, P(), P(("z", "y"), "h", None)),
        out_specs=(rows,) * 4,
        check_vma=False,
    )
```
